128 devices in a mesh: gx: 8 (over x, y_hi), gy: 16 (over z, y_lo, core).
Axes of the slice: x: 4, y: 4 (y_hi: 2, y_lo: 2; y = y_hi * 2 + y_lo), z: 4, core: 2. Of those that a mesh axis runs over, the one named last changes fastest.
Arguments:
- basis: float32 [1, 32, 64, 128, 128], P(None, 'gx', 'gy'), may hold values from 0 to 1, as said below
- trans: float32 [3, 1, 2048, 4096], P(None, None, 'gx', 'gy'), may hold values from 0.05 to 0.5
- reaction: float32 [1, 2048, 4096], P(None, 'gx', 'gy'), may hold values from 0.01 to 0.2
- support: int32 [32, 64, 128, 128], P('gx', 'gy'), may hold values from 0 to 1, as said below
- codes: int32 [32, 64, 128, 128], P('gx', 'gy'), may hold values from 0 to 8, as said below
- active: int32 [1, 32, 64, 128, 128], P(None, 'gx', 'gy'), may hold values from 0 to 1, as said below
- owner: int32 [2048, 1], P(('gx', 'gy')), may hold values from 0 to 7; in each aligned block of 16 rows (0 to 15, 16 to 31, ...) at most 4 rows name the same one
Outputs:
- smoothed: float32 [1, 32, 64, 128, 128], P(None, 'gx', 'gy')
- coarse_rows: float32 [4096, 9], P(('gx', 'gy'))
The draws below stay inside these ranges and needn't reach their ends.
Inputs may be any that keep to these rules, and one draw needn't show every extreme that they name: `support`: 1 on every cell inside the grid that codes marks 4; 0 on each window's outermost cycle of cells and outside the grid. `codes`: inside the grid, (dx + 1) * 3 + (dy + 1), where (dx, dy) is the offset of the coarse block holding the cell from the window's own block, the same block for a cell in every window; 4 outside the grid. `active`: the same for a cell in every window that holds it; 0 outside the grid. `basis`: nonnegative; 0 wherever support or active is 0; positive on the active cells that codes marks 4. The coarse blocks of one device name each owner at most 4 times.
All inputs are finite; a program needn't handle non-finite values.
Results may differ from the reference program's by a relative error of at most 0.0003.
Values sent between devices are 32-bit elements; how exact they have to be, the bound alone decides.
A program may use at most 128 MiB of HBM per device.

```python
import math
import jax
import jax.numpy as jnp
import numpy as np
from jax import lax

B = 64
BX = 4
BY = 4
NL = 1
ITERS = 3
CBX = 32
CBY = 64
NX = 2048
NY = 4096
NBLK = 2048
CAP = 4
N_GX = 8
N_GY = 16


def cut_windows(whole, count_x, count_y, block_width):
    leading = whole.shape[:-2]
    pieces = whole.reshape(leading + (count_x + 1, block_width, count_y + 1, block_width))
    row_pairs = jnp.concatenate([pieces[..., :-1, :, :, :], pieces[..., 1:, :, :, :]], axis=-3)
    paired = jnp.concatenate([row_pairs[..., :-1, :], row_pairs[..., 1:, :]], axis=-1)
    return jnp.swapaxes(paired, -3, -2)


def layout(key):
    margin = B // 2
    jitter = B // 8
    key_first, key_second, key_reach, key_live = jax.random.split(key, 4)
    first_pos = jnp.arange(NX, dtype=jnp.int32)[:, None]
    second_pos = jnp.arange(NY, dtype=jnp.int32)[None, :]
    block_first = jnp.clip((first_pos + jax.random.randint(key_first, (NX, NY), -jitter, jitter + 1)) // B, 0, CBX - 1)
    block_second = jnp.clip((second_pos + jax.random.randint(key_second, (NX, NY), -jitter, jitter + 1)) // B, 0, CBY - 1)
    inside = cut_windows(jnp.pad(jnp.ones((NX, NY), jnp.int32), margin), CBX, CBY, B)
    win_first = cut_windows(jnp.pad(block_first, margin), CBX, CBY, B)
    win_second = cut_windows(jnp.pad(block_second, margin), CBX, CBY, B)
    home_first = jnp.arange(CBX, dtype=jnp.int32)[:, None, None, None]
    home_second = jnp.arange(CBY, dtype=jnp.int32)[None, :, None, None]
    offset_code = (win_first - home_first + 1) * 3 + (win_second - home_second + 1)
    block_codes = jnp.where(inside == 1, offset_code, 4).astype(jnp.int32)
    cell_pos = jnp.arange(2 * B, dtype=jnp.int32)
    apart = jnp.maximum(jnp.maximum(margin - cell_pos, cell_pos - (margin + B - 1)), 0)
    apart = jnp.maximum(apart[:, None], apart[None, :])
    reach = jax.random.randint(key_reach, (NX + B, NY + B), margin // 2, margin)
    reach_win = cut_windows(reach, CBX, CBY, B)
    near = jnp.where((block_codes == 4) | (apart[None, None] <= reach_win), 1, 0)
    support_mask = (inside * near).astype(jnp.int32)
    live = jnp.where(jax.random.randint(key_live, (NL, NX, NY), 0, 8) > 0, 1, 0).astype(jnp.int32)
    live_win = cut_windows(jnp.pad(live, ((0, 0), (margin, margin), (margin, margin))), CBX, CBY, B)
    return (block_codes, support_mask, live_win)


def draw_support(key, part):
    block_codes, support_mask, live_win = layout(key)
    return support_mask


def draw_codes(key, part):
    block_codes, support_mask, live_win = layout(key)
    return block_codes


def draw_active(key, part):
    block_codes, support_mask, live_win = layout(key)
    return live_win


def draw_basis(key, part):
    block_codes, support_mask, live_win = layout(key)
    key = jax.random.fold_in(key, 4)
    kept = (support_mask[None] * live_win).astype(jnp.float32)
    uniform_values = jax.random.uniform(key, kept.shape, jnp.float32, 0.0, 1.0)
    values_out = 0.2 + 0.8 * uniform_values
    return values_out * kept


def block_scale(own_key, dims, cuts, smallest, top_value):
    def one(dim, blocks):
        draws = jax.random.uniform(jax.random.fold_in(jax.random.fold_in(own_key, 6), dim), (blocks,), jnp.float32, smallest / len(cuts), top_value / len(cuts))
        return jnp.repeat(jnp.exp(draws), dims[dim] // blocks).reshape((-1,) + (1,) * (len(dims) - dim - 1))

    loudness = one(*cuts[0])
    for cut in cuts[1:]:
        loudness = loudness * one(*cut)
    return loudness


def shared_out(key, own, number, rows, number_of, top, most, slope):
    sequence = jax.random.permutation(key, number_of)
    crowded, common = load_shares(number_of, rows * top, most, slope, True), load_shares(number_of, rows * top, most, slope, False)
    places = jnp.arange(number_of)

    def named(sizes, rotation):
        used = int((sizes > 0).sum())
        fixed = max(1, used // 4)
        shifted = fixed + (places - fixed + rotation * (used - fixed)) % max(1, number_of - fixed)
        return jnp.zeros((number_of,), jnp.int32).at[sequence[jnp.where(places < fixed, places, shifted)]].set(jnp.asarray(sizes, jnp.int32))

    sizes = jnp.where(number % 4 == 0, named(crowded, number // 4), named(common, number - number // 4 - 1))
    mixed = jax.random.permutation(jax.random.fold_in(own, 3), number_of)
    source_of, sink = mixed[0:number_of // 2 * 2:2], mixed[1:number_of // 2 * 2:2]
    room = jnp.minimum(sizes[source_of] - 1, most - sizes[sink]) // 2
    room = jnp.where((source_of == sequence[0]) | (sink == sequence[0]) | (sizes[sink] == 0), 0, jnp.maximum(room, 0))
    shifted = jax.random.randint(jax.random.fold_in(own, 4), (number_of // 2,), 0, 1 << 20) % (room + 1)
    sizes = sizes.at[source_of].add(-shifted).at[sink].add(shifted)
    labels = jnp.searchsorted(jnp.cumsum(sizes), jnp.arange(rows * top), side="right").astype(jnp.int32)
    listing = labels.reshape(top, rows).T
    listing = listing[jax.random.permutation(jax.random.fold_in(own, 1), rows)]
    rotation = jax.random.randint(jax.random.fold_in(own, 2), (rows, 1), 0, top)
    return jnp.take_along_axis(listing, (jnp.arange(top)[None, :] + rotation) % top, axis=1)


def load_shares(amount, total, limit, slope, full):
    portions = [(1 << 20) // math.isqrt(grade ** slope) + 1 for grade in range(1, amount + 1)]
    largest = limit if full else min(limit, max(-(-total // amount), total * portions[0] // sum(portions)))
    least = 1 if total - largest >= amount - 1 else 0
    counts, surplus = [largest] + [least] * (amount - 1), total - largest - least * (amount - 1)
    while surplus > 0:
        candidates = [i for i in range(1, amount) if counts[i] < largest] or [i for i in range(1, amount) if counts[i] < limit]
        pool, left = sum([portions[i] for i in candidates]), surplus
        for i in candidates:
            addition = min(limit - counts[i], max(1, left * portions[i] // pool), surplus)
            counts[i] = counts[i] + addition
            surplus = surplus - addition
    return np.array(counts)


def setup_inputs(seed: int = 0) -> dict:
    key_of = jax.random.split(jax.random.key(seed), 8)
    basis = draw_basis(jax.random.fold_in(key_of[7], 71), 0)
    trans = jnp.clip(jnp.exp(math.log(0.5) - 2.3025851 * jax.random.uniform(key_of[1], (3, NL, NX, NY), jnp.float32) ** block_scale(key_of[1], (3, NL, NX, NY), ((2, 8), (3, 16)), -0.2, 0.2)), 0.05, 0.5)
    reaction = jnp.clip(jnp.exp(math.log(0.2) - 2.9957323 * jax.random.uniform(key_of[2], (NL, NX, NY), jnp.float32) ** block_scale(key_of[2], (NL, NX, NY), ((1, 8), (2, 16)), -0.2, 0.2)), 0.01, 0.2)
    support = draw_support(jax.random.fold_in(key_of[7], 71), 0)
    codes = draw_codes(jax.random.fold_in(key_of[7], 71), 0)
    active = draw_active(jax.random.fold_in(key_of[7], 71), 0)
    owner_keys = jax.random.split(jax.random.fold_in(key_of[6], 1), NBLK // (BX * BY))
    owner_turns = jax.random.permutation(jax.random.fold_in(key_of[6], 3), NBLK // (BX * BY))
    owner = jax.vmap(lambda own, number: shared_out(jax.random.fold_in(key_of[6], 2), own, number, BX * BY, N_GX, 1, CAP, 2))(owner_keys, owner_turns).reshape((NBLK, 1))
    return dict(basis=basis, trans=trans, reaction=reaction, support=support, codes=codes, active=active, owner=owner)


relaxation = 2.0 / 3.0


def strip_windows(strip, count_y, block_width):
    leading = strip.shape[:-1]
    pieces = strip.reshape(leading + (count_y + 1, block_width))
    paired = jnp.concatenate([pieces[..., :-1, :], pieces[..., 1:, :]], axis=-1)
    return jnp.swapaxes(paired, -3, -2)


def spread_windows(blocks, count_x, count_y, block_width):
    leading = blocks.shape[:-4]
    summed = None
    for half_x in range(2):
        for half_y in range(2):
            quarter = blocks[..., half_x * block_width:(half_x + 1) * block_width, half_y * block_width:(half_y + 1) * block_width]
            widths = [(0, 0)] * len(leading) + [(half_x, 1 - half_x), (half_y, 1 - half_y), (0, 0), (0, 0)]
            placed = jnp.pad(quarter, widths)
            summed = placed if summed is None else summed + placed
    summed = jnp.swapaxes(summed, -3, -2)
    return summed.reshape(leading + ((count_x + 1) * block_width, (count_y + 1) * block_width))


def next_cell(cell_values, along):
    extent = cell_values.shape[along]
    upper_part = lax.slice_in_dim(cell_values, 1, extent, axis=along)
    return jnp.concatenate([upper_part, jnp.zeros_like(lax.slice_in_dim(cell_values, 0, 1, axis=along))], axis=along)


def prior_cell(cell_values, along):
    extent = cell_values.shape[along]
    lower_part = lax.slice_in_dim(cell_values, 0, extent - 1, axis=along)
    return jnp.concatenate([jnp.zeros_like(lax.slice_in_dim(cell_values, 0, 1, axis=along)), lower_part], axis=along)


def operate(cell_values, trans_win, reaction_win):
    dims_count = cell_values.ndim
    result = reaction_win * cell_values
    for face_index, along in ((0, dims_count - 2), (1, dims_count - 1), (2, 0)):
        face_flux = trans_win[face_index] * (cell_values - next_cell(cell_values, along))
        result = result + face_flux - prior_cell(face_flux, along)
    return result


def diagonal_scale(trans_win, reaction_win):
    dims_count = reaction_win.ndim
    summed = reaction_win
    for face_index, along in ((0, dims_count - 2), (1, dims_count - 1), (2, 0)):
        summed = summed + trans_win[face_index] + prior_cell(trans_win[face_index], along)
    return summed


def assemble_rows(column_halo, count_x, count_y):
    picked = []
    for code in range(9):
        shift_x = code // 3 - 1
        shift_y = code % 3 - 1
        picked.append(column_halo[8 - code, 1 + shift_x:1 + shift_x + count_x, 1 + shift_y:1 + shift_y + count_y])
    return jnp.stack(picked, axis=-1)


def ranks(owners):
    count_rows = owners.shape[0]
    same_owner = owners[:, None] == owners[None, :]
    earlier = jnp.arange(count_rows)[None, :] < jnp.arange(count_rows)[:, None]
    return jnp.sum(jnp.where(same_owner & earlier, 1, 0), axis=1).astype(jnp.int32)


def reference(basis, trans, reaction, support, codes, active, owner):
    margin = B // 2
    trans_pad = jnp.pad(trans, ((0, 0), (0, 0), (margin, margin), (margin, margin)))
    reaction_pad = jnp.pad(reaction, ((0, 0), (margin, margin), (margin, margin)))
    row_ids = jnp.arange(CBX, dtype=jnp.int32)

    def coefficient_row(row_index):
        trans_row = strip_windows(lax.dynamic_slice_in_dim(trans_pad, row_index * B, 2 * B, axis=2), CBY, B)
        reaction_row = strip_windows(lax.dynamic_slice_in_dim(reaction_pad, row_index * B, 2 * B, axis=1), CBY, B)
        live = lax.dynamic_index_in_dim(active, row_index, axis=1, keepdims=False).astype(jnp.float32)
        return trans_row, reaction_row, live

    current = basis
    for sweep in range(ITERS):
        def relax_row(row_index):
            trans_row, reaction_row, live = coefficient_row(row_index)
            kept = lax.dynamic_index_in_dim(support, row_index, axis=0, keepdims=False).astype(jnp.float32)[None] * live
            scale = diagonal_scale(trans_row, reaction_row) + 1.0 - live
            block_row = lax.dynamic_index_in_dim(current, row_index, axis=1, keepdims=False)
            return kept * (block_row - relaxation * operate(block_row, trans_row, reaction_row) / scale)

        raw = jnp.moveaxis(lax.map(relax_row, row_ids), 0, 1)
        totals = spread_windows(raw, CBX, CBY, B)

        def normal_row(row_index):
            total_row = strip_windows(lax.dynamic_slice_in_dim(totals, row_index * B, 2 * B, axis=1), CBY, B)
            live = lax.dynamic_index_in_dim(active, row_index, axis=1, keepdims=False).astype(jnp.float32)
            return lax.dynamic_index_in_dim(raw, row_index, axis=1, keepdims=False) / (total_row + 1.0 - live)

        current = jnp.moveaxis(lax.map(normal_row, row_ids), 0, 1)

    def column_row(row_index):
        trans_row, reaction_row, live = coefficient_row(row_index)
        applied = operate(lax.dynamic_index_in_dim(current, row_index, axis=1, keepdims=False), trans_row, reaction_row)
        weighted = jnp.sum(applied * live, axis=0)
        code_row = lax.dynamic_index_in_dim(codes, row_index, axis=0, keepdims=False)
        sums = [jnp.sum(jnp.where(code_row == code, weighted, 0.0), axis=(1, 2)) for code in range(9)]
        return jnp.stack(sums, axis=0) / (B * NL)

    columns = jnp.moveaxis(lax.map(column_row, row_ids), 0, 1)
    padded = jnp.pad(columns, ((0, 0), (1, 1), (1, 1)))
    coarse = assemble_rows(padded, CBX, CBY)
    by_device = coarse.reshape(N_GX, BX, N_GY, BY, 9).transpose(0, 2, 1, 3, 4).reshape(N_GX * N_GY, BX * BY, 9)
    owners = owner.reshape(N_GX * N_GY, BX * BY)
    order_rank = jax.vmap(ranks)(owners)
    device_ids = jnp.arange(N_GX * N_GY, dtype=jnp.int32)[:, None]
    source_x = device_ids // N_GY
    source_y = device_ids % N_GY
    target = ((owners * N_GY + source_y) * N_GX + source_x) * CAP + order_rank
    result = jnp.zeros((N_GX * N_GY * N_GX * CAP, 9), jnp.float32).at[target.reshape(-1)].set(by_device.reshape(-1, 9))
    return current, result
```

```python
import jax
import jax.numpy as jnp
from jax import lax
from jax.experimental import pallas as pl
from jax.experimental.pallas import tpu as pltpu
from jax.sharding import PartitionSpec as P

MESH = pl.DeviceIdType.MESH
OMEGA = 2.0 / 3.0
NGX, NGY = 8, 16
ROWS = 288
SLABS = 34
F32 = jnp.float32
YROWS = 608
P0 = 320


def lanes():
    return lax.broadcasted_iota(jnp.int32, (8, 128), 1)


def subs():
    return lax.broadcasted_iota(jnp.int32, (8, 128), 0)


def roll(x, shift):
    shift = shift % 128
    return x if shift == 0 else pltpu.roll(x, shift, 1)


def sroll(x, shift):
    shift = shift % 8
    return x if shift == 0 else pltpu.roll(x, shift, 0)


def flip(x):
    return pltpu.roll(x, 64, 1)


def fold_rows(parts):
    sub = subs()
    step = 1
    while len(parts) > 1:
        low = (sub // step) % 2 == 0
        merged = []
        for i in range(0, len(parts), 2):
            a, b = parts[i], parts[i + 1]
            merged.append(jnp.where(low, a, sroll(b, step)) + jnp.where(low, sroll(a, -step), b))
        parts = merged
        step *= 2
    return parts[0]


def kernel(
    basis, trans, reaction, support, codes, active, owner,
    out, rows_out,
    va, vb, sup, act, cod, tr, re, tx, ty, tyw, dg, kd, k4, ia, hc, ds, dsup,
    ys, yl, rs, rl, tb, cls, zz,
    lsem, ssem, rsem, s2, r2, st, rt,
):
    gx = lax.axis_index("gx")
    gy = lax.axis_index("gy")

    def exists(dx, dy):
        return (gx + dx >= 0) & (gx + dx < NGX) & (gy + dy >= 0) & (gy + dy < NGY)

    bar = pltpu.get_barrier_semaphore()
    peers = [(s, t) for t in (-1, 0, 1) for s in range(NGX) if (s, t) != (0, 0)]
    for s, t in peers:
        @pl.when(exists(0, t))
        def _(s=s, t=t):
            pl.semaphore_signal(bar, inc=1, device_id=((gx + s) % NGX, gy + t), device_id_type=MESH)

    loads = []

    def load(src, dst):
        c = pltpu.make_async_copy(src, dst, lsem.at[len(loads)])
        c.start()
        loads.append(c)

    wins = ((0, 24, 128, 0), (1, 0, 128, 1), (2, 0, 128, 0), (3, 0, 104, 1))
    for j, lo, hi, px in wins:
        at = 64 * j - 32 + lo + 16
        load(basis.at[j, :, pl.ds(lo, hi - lo), :], va.at[px, pl.ds(0, 4), pl.ds(at, hi - lo), :])
        load(support.at[j, :, pl.ds(lo, hi - lo), :], sup.at[px, :, pl.ds(at, hi - lo), :])
    for i, (j, lo) in enumerate(((0, 0), (3, 88))):
        load(basis.at[j, :, pl.ds(lo, 40), :], ds.at[i])
        load(support.at[j, :, pl.ds(lo, 40), :], dsup.at[i])
    load(trans, tr.at[:, pl.ds(16, 256), :])
    load(reaction, re.at[pl.ds(16, 256), :])
    n_first = len(loads)
    for j, lo, hi in ((0, 24, 128), (2, 0, 128), (3, 64, 104)):
        at = 64 * j - 32 + lo + 16
        load(active.at[j, :, pl.ds(lo, hi - lo), :], act.at[:, pl.ds(at, hi - lo), :])
        load(codes.at[j, :, pl.ds(lo, hi - lo), :], cod.at[:, pl.ds(at, hi - lo), :])

    zero = jnp.zeros((8, 128), F32)
    for buf in (va, vb):
        for px in range(2):
            for kt in range(5):
                buf[px, kt, 0:8, :] = zero
                buf[px, kt, 280:288, :] = zero
    for kt in range(5):
        tx[kt, 0:8, :] = zero

    for dx in (1, -1):
        @pl.when(jnp.logical_not(exists(-dx, 0)))
        def _(dx=dx):
            px, at, ring, j, lo = (1, 8, 8, 3, 0) if dx == 1 else (0, 240, 272, 0, 0)
            for kt in range(4):
                va[px, kt, at:at + 40, :] = jnp.zeros((40, 128), F32)
                sup[px, kt, at:at + 40, :] = jnp.zeros((40, 128), jnp.int32)
            for f in range(3):
                tr[f, ring:ring + 8, :] = jnp.zeros((8, 256), F32)
            re[ring:ring + 8, :] = jnp.zeros((8, 256), F32)
            jo, ro = (0, 0) if dx == 1 else (3, 96)
            for k in range(4):
                out[jo, k, ro:ro + 32, :] = jnp.zeros((32, 128), F32)
    for dy, side in ((1, 0), (-1, 1)):
        @pl.when(jnp.logical_not(exists(0, -dy)))
        def _(side=side, dy=dy):
            yl[side, 48:560, :] = jnp.zeros((512, 128), F32)
            rl[side, 8:120, :] = jnp.zeros((112, 128), F32)
            for s in range(NGX):
                tb[1 - dy, s] = jnp.zeros((16, 128), F32)
        for dx in (1, -1):
            @pl.when(jnp.logical_not(exists(-dx, -dy)))
            def _(side=side, dx=dx):
                at = 0 if dx == 1 else 560
                yl[side, at:at + 48, :] = jnp.zeros((48, 128), F32)
                at = 120 if dx == 1 else 0
                rl[side, at:at + 8, :] = jnp.zeros((8, 128), F32)

    n_peers = 7 + NGX * (jnp.where(exists(0, -1), 1, 0) + jnp.where(exists(0, 1), 1, 0))
    pl.semaphore_wait(bar, n_peers)

    def remote(dx, dy, src, dst, i):
        return pltpu.make_async_remote_copy(
            src, dst, ssem.at[i], rsem.at[i], device_id=(gx + dx, gy + dy), device_id_type=MESH
        )

    def x_copies(dx):
        if dx == 1:
            j, lo, px, at, src_ring, dst_ring, i = 3, 88, 1, 8, 248, 8, 0
        else:
            j, lo, px, at, src_ring, dst_ring, i = 0, 0, 0, 240, 0, 272, 4
        return [
            remote(dx, 0, basis.at[j, :, pl.ds(lo, 40), :], va.at[px, pl.ds(0, 4), pl.ds(at, 40), :], i),
            remote(dx, 0, support.at[j, :, pl.ds(lo, 40), :], sup.at[px, :, pl.ds(at, 40), :], i + 1),
            remote(dx, 0, trans.at[:, pl.ds(src_ring, 8), :], tr.at[:, pl.ds(dst_ring, 8), :], i + 2),
            remote(dx, 0, reaction.at[pl.ds(src_ring, 8), :], re.at[pl.ds(dst_ring, 8), :], i + 3),
        ]

    def y_copy(dx, dy):
        side = 0 if dy == 1 else 1
        at, n = {0: (48, 512), 1: (0, 48), -1: (560, 48)}[dx]
        i = 8 + {0: 0, 1: 1, -1: 2}[dx] * 2 + side
        return [remote(dx, dy, ys.at[side, pl.ds(at, n), :], yl.at[side, pl.ds(at, n), :], i)]

    sends = [((dx, 0), x_copies(dx)) for dx in (1, -1)]
    for (dx, dy), cs in sends:
        @pl.when(exists(dx, dy))
        def _(cs=cs):
            for c in cs:
                c.start()

    for c in loads[:n_first]:
        c.wait()
    lane = lanes()
    right = lane >= 64

    def combine(i, _):
        r = pl.ds(pl.multiple_of(i * 8, 8), 8)
        re[r, :] = re[r, :] + tr[2, r, :]
        return 0

    lax.fori_loop(2, 34, combine, 0)

    for dx, jj in ((1, 1), (-1, 0)):
        for dy, side, k in ((1, 0, 3), (-1, 1, 0)):
            base = 8 if dx == 1 else 560
            for s in range(5):
                b = ds[jj, k, s * 8:s * 8 + 8, :]
                p = flip(dsup[jj, k, s * 8:s * 8 + 8, :].astype(F32))
                ys[side, base + s * 8:base + s * 8 + 8, :] = (
                    jnp.where(right, b, p) if dy == 1 else jnp.where(right, p, b)
                )
            at = 264 if dx == 1 else 16
            cell = []
            for f in range(3):
                ref = (lambda a, b: tr[f, a, b]) if f < 2 else (lambda a, b: re[a, b])
                x = ref(slice(at, at + 8), slice(128, 256) if dy == 1 else slice(0, 128))
                cell.append(roll(x, (8 + 8 * f) if dy == 1 else 8 * f))
            m = jnp.where(lane < 8, cell[0], jnp.where(lane < 16, cell[1], cell[2]))
            cat = 0 if dx == 1 else 600
            ys[side, cat:cat + 8, :] = m
    for dy in (1, -1):
        for dx in (1, -1):
            sends.append(((dx, dy), y_copy(dx, dy)))
            @pl.when(exists(dx, dy))
            def _(c=sends[-1][1]):
                c[0].start()

    for dy, side, k in ((1, 0, 3), (-1, 1, 0)):
        def pack(i, _, dy=dy, side=side, k=k):
            for px in range(2):
                src = pl.multiple_of(i * 8 + (8 if px == 0 else 48), 8)
                dst = pl.multiple_of(i * 8 + (8 + P0 if px == 0 else 48), 8)
                b = va[px, k, pl.ds(src, 8), :]
                p = flip(sup[px, k, pl.ds(src, 8), :].astype(F32))
                ys[side, pl.ds(dst, 8), :] = jnp.where(right, b, p) if dy == 1 else jnp.where(right, p, b)
            return 0

        lax.fori_loop(0, 29, pack, 0)
        for f in range(3):
            for h in range(2):
                m = None
                for i in range(16):
                    at = 16 + h * 128 + i * 8
                    col = slice(128, 256) if dy == 1 else slice(0, 128)
                    x = tr[f, at:at + 8, col] if f < 2 else re[at:at + 8, col]
                    x = roll(x, (8 * i + 8) if dy == 1 else 8 * i)
                    m = x if m is None else jnp.where(lane < 8 * i, m, x)
                at = 280 + (f * 2 + h) * 8
                ys[side, at:at + 8, :] = m
        sends.append(((0, dy), y_copy(0, dy)))
        @pl.when(exists(0, dy))
        def _(c=sends[-1][1]):
            c[0].start()

    for c in loads[n_first:]:
        c.wait()

    sub = subs()
    block = jnp.where(
        (sub >= 1) & (sub <= 4) & (lane >= 16) & (lane < 80), (sub - 1) * 4 + lane // 16 - 1, -1
    )
    own_of = jnp.full((8, 128), -1, jnp.int32)
    for n in range(16):
        own_of = jnp.where(block == n, owner[n], own_of)
    place = jnp.zeros((8, 128), jnp.int32)
    for n in range(16):
        place = place + jnp.where((own_of == owner[n]) & (block > n), 1, 0)
    target = jnp.where(block >= 0, own_of * 4 + place, -1).astype(F32)

    for (dx, dy), cs in sends:
        @pl.when(exists(-dx, -dy))
        def _(cs=cs):
            for c in cs:
                c.wait_recv()
    for at in (8, 272):
        re[at:at + 8, :] = re[at:at + 8, :] + tr[2, at:at + 8, :]

    for side in range(2):
        to = 24 if side == 0 else 96
        for f in range(3):
            for s in range(SLABS):
                if s == 0 or s == SLABS - 1:
                    at = 0 if s == 0 else 600
                    x = roll(yl[side, at:at + 8, :], to - 8 * f)
                else:
                    h, i = divmod(s - 1, 16)
                    at = 280 + (f * 2 + h) * 8
                    x = roll(yl[side, at:at + 8, :], to - 8 * i)
                hc[side, f, s * 8:s * 8 + 8, :] = x

    def spread(t0, t1, left, rite):
        r0, l0, r1, l1 = roll(t0, 32), roll(t0, -32), roll(t1, 32), roll(t1, -32)
        k0 = jnp.where(lane < 24, 0.0, jnp.where(lane < 32, left, r0))
        k1 = jnp.where(lane < 96, l0, l1)
        k2 = jnp.where(lane < 32, r0, r1)
        k3 = jnp.where(lane < 96, l1, jnp.where(lane < 104, rite, 0.0))
        return [k0, k1, k2, k3, jnp.where(right, flip(k0), flip(k3))]

    def prepare(i, _):
        r = pl.ds(pl.multiple_of(i * 8 + 8, 8), 8)
        h = pl.ds(pl.multiple_of(i * 8, 8), 8)
        cx = spread(tr[0, r, 0:128], tr[0, r, 128:256], hc[0, 0, h, :], hc[1, 0, h, :])
        cy = spread(tr[1, r, 0:128], tr[1, r, 128:256], hc[0, 1, h, :], hc[1, 1, h, :])
        cr = spread(re[r, 0:128], re[r, 128:256], hc[0, 2, h, :], hc[1, 2, h, :])
        live = [act[k, r, :].astype(F32) for k in range(4)]
        live.append(jnp.where(right, flip(live[0]), flip(live[3])))
        for kt in range(5):
            tx[kt, r, :] = cx[kt]
            ty[kt, r, :] = cy[kt]
            w = pltpu.roll(cy[kt], 1, 1)
            tyw[kt, r, :] = w
            prev = tx[kt, pl.ds(i * 8 + 7, 8), :]
            d = cr[kt] + cx[kt] + prev + cy[kt] + w
            dg[kt, r, :] = d
            wd = OMEGA / jnp.maximum(d, 0.005)
            ia[kt, r, :] = 1.0 - live[kt]
            for px in range(2):
                if kt < 4:
                    kept = sup[px, kt, r, :].astype(F32) * live[kt]
                else:
                    yr = pl.ds(pl.multiple_of(i * 8 + 8 + (P0 if px == 0 else 0), 8), 8)
                    from_low, from_high = yl[0, yr, :], yl[1, yr, :]
                    va[px, 4, r, :] = jnp.where(right, from_low, from_high)
                    kept = flip(jnp.where(right, from_high, from_low)) * live[4]
                kd[px, kt, r, :] = wd * kept
        return 0

    lax.fori_loop(0, SLABS, prepare, 0)

    low_x, high_x = gx == 0, gx == NGX - 1
    low_y, high_y = gy == 0, gy == NGY - 1

    def classify(i, _):
        r = pl.ds(pl.multiple_of(i * 8 + 16, 8), 8)
        h = i // 4
        thx = jnp.where((h == 0) | (h == 3) | (h == 4), 3, 6)
        thx = jnp.where((h == 0) & low_x, 6, thx)
        thx = jnp.where((h == 7) & high_x, 3, thx)
        got = []
        for k in range(4):
            c = cod[k, r, :]
            cy = c - 3 * (jnp.where(c >= 3, 1, 0) + jnp.where(c >= 6, 1, 0))
            thl = jnp.where(low_y, 2, 1) if k == 0 else 1
            thr = jnp.where(high_y, 1, 2) if k == 3 else 2
            thy = jnp.where(right, thr, thl)
            v = jnp.where(c >= thx, 2, 0) + jnp.where(cy >= thy, 1, 0)
            got.append(jnp.where(act[k, r, :] > 0, v, 4))
        k4 = jnp.where(right, flip(got[0]), flip(got[3]))
        cls[0, r, :] = jnp.where(lane >= 32, got[0], 4)
        cls[1, r, :] = got[1]
        cls[2, r, :] = got[2]
        cls[3, r, :] = jnp.where(lane < 96, got[3], 4)
        cls[4, r, :] = jnp.where((lane < 32) | (lane >= 96), k4, 4)
        return 0

    lax.fori_loop(0, 32, classify, 0)

    def flux_sum(v, px, kt, i):
        r = pl.ds(pl.multiple_of(i * 8 + 8, 8), 8)
        mid = v[px, kt, r, :]
        up = v[px, kt, pl.ds(i * 8 + 9, 8), :]
        dn = v[px, kt, pl.ds(i * 8 + 7, 8), :]
        total = (
            tx[kt, r, :] * up
            + tx[kt, pl.ds(i * 8 + 7, 8), :] * dn
            + ty[kt, r, :] * pltpu.roll(mid, 127, 1)
            + tyw[kt, r, :] * pltpu.roll(mid, 1, 1)
        )
        return mid, total

    def sweep(src, dst):
        def body(i, _):
            r = pl.ds(pl.multiple_of(i * 8 + 8, 8), 8)
            raw = [[None] * 5 for _ in range(2)]
            for kt in range(5):
                for px in range(2):
                    mid, total = flux_sum(src, px, kt, i)
                    raw[px][kt] = (1.0 - OMEGA) * mid + kd[px, kt, r, :] * total
            both = [raw[0][kt] + raw[1][kt] for kt in range(5)]
            turned = [flip(b) for b in both]
            for kt in range(5):
                t = both[kt] + jnp.where(right, turned[(kt + 1) % 5], turned[(kt + 4) % 5])
                t = jnp.maximum(t + ia[kt, r, :], 1e-30)
                inv = 1.0 / t
                for px in range(2):
                    dst[px, kt, r, :] = raw[px][kt] * inv
            return 0

        lax.fori_loop(0, SLABS, body, 0)

    sweep(va, vb)
    sweep(vb, va)
    sweep(va, vb)
    fin = vb

    for side in range(2):
        def place_lanes(xs, side=side):
            m = None
            for g, x in enumerate(xs):
                x = roll(x, 32 * g if side == 0 else 32 * g + 32)
                m = x if m is None else jnp.where(lane < 32 * g, m, x)
            return m

        rs[side, 0:8, :] = place_lanes([fin[1, 4, 16 + 8 * g:24 + 8 * g, :] for g in range(4)])
        rs[side, 120:128, :] = place_lanes([fin[0, 4, 240 + 8 * g:248 + 8 * g, :] for g in range(4)])

        def pack_back(i, _, side=side, place_lanes=place_lanes):
            def at(px, first):
                return fin[px, 4, pl.ds(pl.multiple_of(first + i * 8, 8), 8), :]

            rs[side, pl.ds(pl.multiple_of(8 + i * 8, 8), 8), :] = place_lanes(
                [at(0, 16), at(0, 16 + 112), at(1, 48), at(1, 48 + 112)]
            )
            return 0

        lax.fori_loop(0, 14, pack_back, 0)

    def remote2(dx, dy, src, dst, i):
        return pltpu.make_async_remote_copy(
            src, dst, s2.at[i], r2.at[i], device_id=(gx + dx, gy + dy), device_id_type=MESH
        )

    backs = [
        ((-1, 0), remote2(-1, 0, fin.at[1, pl.ds(0, 4), pl.ds(16, 32), :], out.at[3, :, pl.ds(96, 32), :], 0)),
        ((1, 0), remote2(1, 0, fin.at[0, pl.ds(0, 4), pl.ds(240, 32), :], out.at[0, :, pl.ds(0, 32), :], 1)),
    ]
    for dx in (0, 1, -1):
        for dy, side in ((1, 0), (-1, 1)):
            at, n = {0: (8, 112), 1: (120, 8), -1: (0, 8)}[dx]
            i = 2 + {0: 0, 1: 1, -1: 2}[dx] * 2 + side
            backs.append(
                ((dx, dy), remote2(dx, dy, rs.at[side, pl.ds(at, n), :], rl.at[side, pl.ds(at, n), :], i))
            )
    for (dx, dy), c in backs:
        @pl.when(exists(dx, dy))
        def _(c=c):
            c.start()

    def image(h, _):
        for kt in range(5):
            acc = [None] * 8
            for s in range(4):
                i = h * 4 + s + 1
                r = pl.ds(pl.multiple_of(i * 8 + 8, 8), 8)
                c = cls[kt, r, :]
                pick = [c == q for q in range(4)]
                for px in range(2):
                    mid, total = flux_sum(fin, px, kt, i)
                    img = dg[kt, r, :] * mid - total
                    for q in range(4):
                        n = (q // 2) * 4 + px * 2 + q % 2
                        x = jnp.where(pick[q], img, 0.0)
                        acc[n] = x if acc[n] is None else acc[n] + x
            zz[h, kt] = fold_rows(acc)
        return 0

    lax.fori_loop(0, 8, image, 0)

    table = jnp.zeros((8, 128), F32)
    bit_x, odd, bit_y = sub // 4, (sub // 2) % 2, sub % 2
    for a in range(5):
        part = jnp.zeros((8, 128), F32)
        base_x = a
        if a == 0:
            base_x = jnp.where(low_x, 1, 0)
        if a == 4:
            base_x = jnp.where(high_x, 3, 4)
        window_x = a - (a + odd) % 2
        dxo = window_x - (base_x - 1 + bit_x)
        for kt in range(5):
            z = zz[0, kt] if a == 0 else (zz[7, kt] if a == 4 else zz[2 * a - 1, kt] + zz[2 * a, kt])
            for shift in (32, 16, 8, 4, 2, 1):
                z = z + roll(z, -shift)
            for half in range(2):
                if kt < 4:
                    b, window_y = kt + half, kt
                else:
                    b, window_y = (4, 4) if half == 0 else (0, -1)
                base_y = b
                if b == 0:
                    base_y = jnp.where(low_y, 1, 0)
                if b == 4:
                    base_y = jnp.where(high_y, 3, 4)
                dyo = window_y - (base_y - 1 + bit_y)
                to = (base_y + bit_y) * 16 + (dxo + 1) * 3 + dyo + 1
                value = jnp.broadcast_to(z[:, 64 * half:64 * half + 1], (8, 128))
                part = part + jnp.where(lane == to, value, 0.0)
        low = jnp.sum(part[0:4], axis=0, keepdims=True)
        high = jnp.sum(part[4:8], axis=0, keepdims=True)
        table = table + jnp.where(sub == base_x, low, 0.0) + jnp.where(sub == base_x + 1, high, 0.0)
    tb[1, gx, 0:8, :] = table * (1.0 / 64.0)
    tb[1, gx, 8:16, :] = target

    hops = []
    for n, (s, t) in enumerate(peers):
        hops.append((t, pltpu.make_async_remote_copy(
            tb.at[1, gx], tb.at[1 - t, gx], st.at[n], rt.at[n],
            device_id=((gx + s) % NGX, gy + t), device_id_type=MESH,
        )))
    for t, c in hops:
        @pl.when(exists(0, t))
        def _(c=c):
            c.start()

    def emit(i, _):
        def one(j, px, first, to):
            for k in range(4):
                out[j, k, pl.ds(pl.multiple_of(to + i * 8, 8), 8), :] = fin[
                    px, k, pl.ds(pl.multiple_of(first + i * 8, 8), 8), :
                ]

        one(0, 0, 16, 32)
        one(1, 1, 48, 0)
        one(2, 0, 112, 0)
        one(3, 1, 176, 0)
        return 0

    lax.fori_loop(0, 12, emit, 0)
    for i in range(12, 16):
        for k in range(4):
            out[1, k, i * 8:i * 8 + 8, :] = fin[1, k, 48 + i * 8:56 + i * 8, :]
            out[2, k, i * 8:i * 8 + 8, :] = fin[0, k, 112 + i * 8:120 + i * 8, :]

    for (dx, dy), c in backs:
        @pl.when(exists(-dx, -dy))
        def _(c=c):
            c.wait_recv()

    for side, k in ((0, 0), (1, 3)):
        def merge(j, at, src, g):
            x = rl[side, pl.ds(src, 8), :]
            x = roll(x, -32 * g if side == 0 else 96 - 32 * g)
            inside = lane < 32 if side == 0 else lane >= 96
            out[j, k, at:at + 8, :] = jnp.where(inside, x, out[j, k, at:at + 8, :])

        for g in range(4):
            merge(0, 8 * g, 120, g)
            merge(3, 96 + 8 * g, 0, g)
        for s in range(28):
            j, at = (0, 32 + 8 * s) if s < 12 else (2, 8 * (s - 12))
            merge(j, at, 8 + 8 * (s % 14), s // 14)
            j, at = (1, 8 * s) if s < 16 else (3, 8 * (s - 16))
            merge(j, at, 8 + 8 * (s % 14), 2 + s // 14)

    for t, c in hops:
        @pl.when(exists(0, -t))
        def _(c=c):
            c.wait_recv()

    joined = []
    for s in range(NGX):
        a = tb[1, s, 0:8, :]
        below = roll(tb[0, s, 0:8, :], -64)
        above = roll(tb[2, s, 0:8, :], 64)
        group = lane // 16
        joined.append(a + jnp.where(group == 1, below, 0.0) + jnp.where(group == 4, above, 0.0))
    for s in range(NGX):
        t = joined[s]
        if s > 0:
            t = t + jnp.where(sub == 1, sroll(joined[s - 1], -4), 0.0)
        if s < NGX - 1:
            t = t + jnp.where(sub == 4, sroll(joined[s + 1], 4), 0.0)
        goal = tb[1, s, 8:16, :]
        for q in range(4):
            mine = jnp.where(goal == (gx * 4 + q).astype(F32), t, 0.0)
            line = jnp.sum(mine, axis=0, keepdims=True)
            line = line + pltpu.roll(line, 96, 1)
            line = line + pltpu.roll(line, 112, 1)
            rows_out[s * 4 + q:s * 4 + q + 1, :] = line[:, 16:25]

    for (dx, dy), cs in sends:
        @pl.when(exists(dx, dy))
        def _(cs=cs):
            for c in cs:
                c.wait_send()
    for (dx, dy), c in backs:
        @pl.when(exists(dx, dy))
        def _(c=c):
            c.wait_send()
    for t, c in hops:
        @pl.when(exists(0, t))
        def _(c=c):
            c.wait_send()


def local(basis, trans, reaction, support, codes, active, owner):
    anywhere = pl.BlockSpec(memory_space=pl.ANY)
    vmem = pl.BlockSpec(memory_space=pltpu.VMEM)
    sem = pltpu.SemaphoreType.DMA
    smoothed, coarse = pl.pallas_call(
        kernel,
        name="smooth",
        out_shape=(
            jax.ShapeDtypeStruct((4, 4, 128, 128), F32),
            jax.ShapeDtypeStruct((32, 9), F32),
        ),
        in_specs=[anywhere] * 6 + [pl.BlockSpec(memory_space=pltpu.SMEM)],
        out_specs=(vmem, vmem),
        scratch_shapes=[
            pltpu.VMEM((2, 5, ROWS, 128), F32),
            pltpu.VMEM((2, 5, ROWS, 128), F32),
            pltpu.VMEM((2, 4, ROWS, 128), jnp.int32),
            pltpu.VMEM((4, ROWS, 128), jnp.int32),
            pltpu.VMEM((4, ROWS, 128), jnp.int32),
            pltpu.VMEM((3, ROWS, 256), F32),
            pltpu.VMEM((ROWS, 256), F32),
            pltpu.VMEM((5, ROWS, 128), F32),
            pltpu.VMEM((5, ROWS, 128), F32),
            pltpu.VMEM((5, ROWS, 128), F32),
            pltpu.VMEM((5, ROWS, 128), F32),
            pltpu.VMEM((2, 5, ROWS, 128), F32),
            pltpu.VMEM((8, 128), F32),
            pltpu.VMEM((5, ROWS, 128), F32),
            pltpu.VMEM((2, 3, 272, 128), F32),
            pltpu.VMEM((2, 4, 40, 128), F32),
            pltpu.VMEM((2, 4, 40, 128), jnp.int32),
            pltpu.VMEM((2, YROWS, 128), F32),
            pltpu.VMEM((2, YROWS, 128), F32),
            pltpu.VMEM((2, 128, 128), F32),
            pltpu.VMEM((2, 128, 128), F32),
            pltpu.VMEM((3, NGX, 16, 128), F32),
            pltpu.VMEM((5, ROWS, 128), jnp.int32),
            pltpu.VMEM((8, 5, 8, 128), F32),
            sem((32,)), sem((16,)), sem((16,)), sem((8,)), sem((8,)), sem((24,)), sem((24,)),
        ],
        compiler_params=pltpu.CompilerParams(
            collective_id=0, has_side_effects=True, vmem_limit_bytes=48 << 20
        ),
    )(basis[0], trans[:, 0], reaction[0], support, codes, active[0], owner.reshape(16))
    return smoothed[None], coarse


def solution(mesh):
    return jax.shard_map(
        local,
        mesh=mesh,
        in_specs=(
            P(None, "gx", "gy", None, None),
            P(None, None, "gx", "gy"),
            P(None, "gx", "gy"),
            P("gx", "gy", None, None),
            P("gx", "gy", None, None),
            P(None, "gx", "gy", None, None),
            P(("gx", "gy"), None),
        ),
        out_specs=(P(None, "gx", "gy", None, None), P(("gx", "gy"), None)),
        check_vma=False,
    )
```

```python
import jax
import jax.numpy as jnp
from jax import lax
from jax.experimental import pallas as pl
from jax.experimental.pallas import tpu as pltpu
from jax.sharding import PartitionSpec as P

MESH = pl.DeviceIdType.MESH
OMEGA = 2.0 / 3.0
NGX, NGY = 8, 16
ROWS = 288
SLABS = 34
F32 = jnp.float32
YROWS = 544
CROWS = 64


def lanes():
    return lax.broadcasted_iota(jnp.int32, (8, 128), 1)


def subs():
    return lax.broadcasted_iota(jnp.int32, (8, 128), 0)


def roll(x, shift):
    shift = shift % 128
    return x if shift == 0 else pltpu.roll(x, shift, 1)


def sroll(x, shift):
    shift = shift % 8
    return x if shift == 0 else pltpu.roll(x, shift, 0)


def flip(x):
    return pltpu.roll(x, 64, 1)


def fold_rows(parts):
    sub = subs()
    step = 1
    while len(parts) > 1:
        low = (sub // step) % 2 == 0
        merged = []
        for i in range(0, len(parts), 2):
            a, b = parts[i], parts[i + 1]
            merged.append(jnp.where(low, a, sroll(b, step)) + jnp.where(low, sroll(a, -step), b))
        parts = merged
        step *= 2
    return parts[0]


def kernel(
    basis, trans, reaction, support, codes, active, owner,
    out, rows_out,
    va, vb, sup, act, cod, tr, re, tx, ty, tyw, dg, kd, ia, hc, ds, dsup,
    ys, yl, yc, yd, rs, rl, tb, cls, zz,
    lsem, ssem, rsem, s2, r2, st, rt,
):
    gx = lax.axis_index("gx")
    gy = lax.axis_index("gy")

    def exists(dx, dy):
        return (gx + dx >= 0) & (gx + dx < NGX) & (gy + dy >= 0) & (gy + dy < NGY)

    bar = pltpu.get_barrier_semaphore()
    peers = [(s, t) for t in (-1, 0, 1) for s in range(NGX) if (s, t) != (0, 0)]
    for s, t in peers:
        @pl.when(exists(0, t))
        def _(s=s, t=t):
            pl.semaphore_signal(bar, inc=1, device_id=((gx + s) % NGX, gy + t), device_id_type=MESH)

    loads = []

    def load(src, dst):
        c = pltpu.make_async_copy(src, dst, lsem.at[len(loads)])
        c.start()
        loads.append(c)

    load(trans, tr.at[:, pl.ds(16, 256), :])
    load(reaction, re.at[pl.ds(16, 256), :])
    n_coef = len(loads)
    wins = ((0, 24, 128, 0), (1, 0, 128, 1), (2, 0, 128, 0), (3, 0, 104, 1))
    for j, lo, hi, px in wins:
        at = 64 * j - 32 + lo + 16
        load(basis.at[j, :, pl.ds(lo, hi - lo), :], va.at[px, pl.ds(0, 4), pl.ds(at, hi - lo), :])
        load(support.at[j, :, pl.ds(lo, hi - lo), :], sup.at[px, :, pl.ds(at, hi - lo), :])
    for i, (j, lo) in enumerate(((0, 0), (3, 88))):
        load(basis.at[j, :, pl.ds(lo, 40), :], ds.at[i])
        load(support.at[j, :, pl.ds(lo, 40), :], dsup.at[i])
    n_first = len(loads)
    for j, lo, hi in ((0, 24, 128), (2, 0, 128), (3, 64, 104)):
        at = 64 * j - 32 + lo + 16
        load(active.at[j, :, pl.ds(lo, hi - lo), :], act.at[:, pl.ds(at, hi - lo), :])
        load(codes.at[j, :, pl.ds(lo, hi - lo), :], cod.at[:, pl.ds(at, hi - lo), :])

    zero = jnp.zeros((8, 128), F32)
    for buf in (va, vb):
        for px in range(2):
            for kt in range(5):
                buf[px, kt, 0:8, :] = zero
                buf[px, kt, 280:288, :] = zero
    for kt in range(5):
        tx[kt, 0:8, :] = zero

    for dx in (1, -1):
        @pl.when(jnp.logical_not(exists(-dx, 0)))
        def _(dx=dx):
            px, at, ring, j, lo = (1, 8, 8, 3, 0) if dx == 1 else (0, 240, 272, 0, 0)
            for kt in range(4):
                va[px, kt, at:at + 40, :] = jnp.zeros((40, 128), F32)
                sup[px, kt, at:at + 40, :] = jnp.zeros((40, 128), jnp.int32)
            for f in range(3):
                tr[f, ring:ring + 8, :] = jnp.zeros((8, 256), F32)
            re[ring:ring + 8, :] = jnp.zeros((8, 256), F32)
            jo, ro = (0, 0) if dx == 1 else (3, 96)
            for k in range(4):
                out[jo, k, ro:ro + 32, :] = jnp.zeros((32, 128), F32)
    for dy, side in ((1, 0), (-1, 1)):
        @pl.when(jnp.logical_not(exists(0, -dy)))
        def _(side=side, dy=dy):
            yl[side, 40:504, :] = jnp.zeros((464, 128), F32)
            yd[side, 8:56, :] = jnp.zeros((48, 128), F32)
            rl[side, 8:120, :] = jnp.zeros((112, 128), F32)
            for s in range(NGX):
                tb[1 - dy, s] = jnp.zeros((16, 128), F32)
        for dx in (1, -1):
            @pl.when(jnp.logical_not(exists(-dx, -dy)))
            def _(side=side, dx=dx):
                at = 0 if dx == 1 else 504
                yl[side, at:at + 40, :] = jnp.zeros((40, 128), F32)
                at = 0 if dx == 1 else 56
                yd[side, at:at + 8, :] = jnp.zeros((8, 128), F32)
                at = 120 if dx == 1 else 0
                rl[side, at:at + 8, :] = jnp.zeros((8, 128), F32)

    lane = lanes()
    sub = subs()
    right = lane >= 64

    for c in loads[:n_coef]:
        c.wait()

    def combine(i, _):
        r = pl.ds(pl.multiple_of(i * 8, 8), 8)
        re[r, :] = re[r, :] + tr[2, r, :]
        return 0

    lax.fori_loop(2, 34, combine, 0, unroll=8)

    def cells(f, at, high):
        col = slice(128, 256) if high else slice(0, 128)
        return tr[f, at:at + 8, col] if f < 2 else re[at:at + 8, col]

    for dy, side in ((1, 0), (-1, 1)):
        high = dy == 1
        for dx, at, to in ((1, 264, 0), (-1, 16, 56)):
            got = [roll(cells(f, at, high), (8 + 8 * f) if high else 8 * f) for f in range(3)]
            yc[side, to:to + 8, :] = jnp.where(lane < 8, got[0], jnp.where(lane < 16, got[1], got[2]))
        for f in range(3):
            for h in range(2):
                m = None
                for i in range(16):
                    x = roll(cells(f, 16 + h * 128 + i * 8, high), (8 * i + 8) if high else 8 * i)
                    m = x if m is None else jnp.where(lane < 8 * i, m, x)
                to = 8 + (f * 2 + h) * 8
                yc[side, to:to + 8, :] = m

    n_peers = 7 + NGX * (jnp.where(exists(0, -1), 1, 0) + jnp.where(exists(0, 1), 1, 0))
    pl.semaphore_wait(bar, n_peers)

    def remote(dx, dy, src, dst, i):
        return pltpu.make_async_remote_copy(
            src, dst, ssem.at[i], rsem.at[i], device_id=(gx + dx, gy + dy), device_id_type=MESH
        )

    def start(d, cs):
        @pl.when(exists(*d))
        def _():
            for c in cs:
                c.start()

    coef_sends, sends = [], []
    for dx in (1, -1):
        src, dst, i = (248, 8, 0) if dx == 1 else (0, 272, 2)
        coef_sends.append(((dx, 0), [
            remote(dx, 0, trans.at[:, pl.ds(src, 8), :], tr.at[:, pl.ds(dst, 8), :], i),
            remote(dx, 0, reaction.at[pl.ds(src, 8), :], re.at[pl.ds(dst, 8), :], i + 1),
        ]))
        start(*coef_sends[-1])
    for dx in (0, 1, -1):
        for dy, side in ((1, 0), (-1, 1)):
            at, n = {0: (8, 48), 1: (0, 8), -1: (56, 8)}[dx]
            i = 4 + {0: 0, 1: 1, -1: 2}[dx] * 2 + side
            coef_sends.append(((dx, dy), [
                remote(dx, dy, yc.at[side, pl.ds(at, n), :], yd.at[side, pl.ds(at, n), :], i)
            ]))
            start(*coef_sends[-1])
    for dx in (1, -1):
        j, lo, px, at, i = (3, 88, 1, 8, 10) if dx == 1 else (0, 0, 0, 240, 12)
        sends.append(((dx, 0), [
            remote(dx, 0, basis.at[j, :, pl.ds(lo, 40), :], va.at[px, pl.ds(0, 4), pl.ds(at, 40), :], i),
            remote(dx, 0, support.at[j, :, pl.ds(lo, 40), :], sup.at[px, :, pl.ds(at, 40), :], i + 1),
        ]))
        start(*sends[-1])

    def y_send(dx, dy, side):
        at, n = {0: (40, 464), 1: (0, 40), -1: (504, 40)}[dx]
        i = 14 + {0: 0, 1: 1, -1: 2}[dx] * 2 + side
        sends.append(((dx, dy), [
            remote(dx, dy, ys.at[side, pl.ds(at, n), :], yl.at[side, pl.ds(at, n), :], i)
        ]))
        start(*sends[-1])

    for c in loads[n_coef:n_first]:
        c.wait()
    for dx, jj in ((1, 1), (-1, 0)):
        for dy, side, k in ((1, 0, 3), (-1, 1, 0)):
            base = 0 if dx == 1 else 504
            for n in range(5):
                b = ds[jj, k, n * 8:n * 8 + 8, :]
                p = flip(dsup[jj, k, n * 8:n * 8 + 8, :].astype(F32))
                ys[side, base + n * 8:base + n * 8 + 8, :] = (
                    jnp.where(right, b, p) if dy == 1 else jnp.where(right, p, b)
                )
            y_send(dx, dy, side)
    for dy, side, k in ((1, 0, 3), (-1, 1, 0)):
        def pack(i, _, dy=dy, side=side, k=k):
            for px in range(2):
                src = pl.multiple_of(i * 8 + (8 if px == 0 else 48), 8)
                dst = pl.multiple_of(i * 8 + (272 if px == 0 else 40), 8)
                b = va[px, k, pl.ds(src, 8), :]
                p = flip(sup[px, k, pl.ds(src, 8), :].astype(F32))
                ys[side, pl.ds(dst, 8), :] = jnp.where(right, b, p) if dy == 1 else jnp.where(right, p, b)
            return 0

        lax.fori_loop(0, 29, pack, 0, unroll=29)
        y_send(0, dy, side)

    for c in loads[n_first:]:
        c.wait()

    block = jnp.where(
        (sub >= 1) & (sub <= 4) & (lane >= 16) & (lane < 80), (sub - 1) * 4 + lane // 16 - 1, -1
    )
    own_of = jnp.full((8, 128), -1, jnp.int32)
    for n in range(16):
        own_of = jnp.where(block == n, owner[n], own_of)
    place = jnp.zeros((8, 128), jnp.int32)
    for n in range(16):
        place = place + jnp.where((own_of == owner[n]) & (block > n), 1, 0)
    target = jnp.where(block >= 0, own_of * 4 + place, -1).astype(F32)

    low_x, high_x = gx == 0, gx == NGX - 1
    low_y, high_y = gy == 0, gy == NGY - 1

    def classify(i, _):
        r = pl.ds(pl.multiple_of(i * 8 + 16, 8), 8)
        h = i // 4
        thx = jnp.where((h == 0) | (h == 3) | (h == 4), 3, 6)
        thx = jnp.where((h == 0) & low_x, 6, thx)
        thx = jnp.where((h == 7) & high_x, 3, thx)
        got = []
        for k in range(4):
            c = cod[k, r, :]
            cy = c - 3 * (jnp.where(c >= 3, 1, 0) + jnp.where(c >= 6, 1, 0))
            thl = jnp.where(low_y, 2, 1) if k == 0 else 1
            thr = jnp.where(high_y, 1, 2) if k == 3 else 2
            thy = jnp.where(right, thr, thl)
            v = jnp.where(c >= thx, 2, 0) + jnp.where(cy >= thy, 1, 0)
            got.append(jnp.where(act[k, r, :] > 0, v, 4))
        k4 = jnp.where(right, flip(got[0]), flip(got[3]))
        cls[0, r, :] = jnp.where(lane >= 32, got[0], 4)
        cls[1, r, :] = got[1]
        cls[2, r, :] = got[2]
        cls[3, r, :] = jnp.where(lane < 96, got[3], 4)
        cls[4, r, :] = jnp.where((lane < 32) | (lane >= 96), k4, 4)
        return 0

    lax.fori_loop(0, 32, classify, 0, unroll=4)

    def arrived(copies):
        for (dx, dy), cs in copies:
            @pl.when(exists(-dx, -dy))
            def _(cs=cs):
                for c in cs:
                    c.wait_recv()

    arrived(coef_sends)
    for at in (8, 272):
        re[at:at + 8, :] = re[at:at + 8, :] + tr[2, at:at + 8, :]
    for side in range(2):
        to = 24 if side == 0 else 96
        for f in range(3):
            for n in range(SLABS):
                if n == 0 or n == SLABS - 1:
                    at = 0 if n == 0 else 56
                    x = roll(yd[side, at:at + 8, :], to - 8 * f)
                else:
                    h, i = divmod(n - 1, 16)
                    at = 8 + (f * 2 + h) * 8
                    x = roll(yd[side, at:at + 8, :], to - 8 * i)
                hc[side, f, n * 8:n * 8 + 8, :] = x

    def spread(t0, t1, left, rite):
        r0, l0, r1, l1 = roll(t0, 32), roll(t0, -32), roll(t1, 32), roll(t1, -32)
        k0 = jnp.where(lane < 24, 0.0, jnp.where(lane < 32, left, r0))
        k1 = jnp.where(lane < 96, l0, l1)
        k2 = jnp.where(lane < 32, r0, r1)
        k3 = jnp.where(lane < 96, l1, jnp.where(lane < 104, rite, 0.0))
        return [k0, k1, k2, k3, jnp.where(right, flip(k0), flip(k3))]

    def widen(i, _):
        r = pl.ds(pl.multiple_of(i * 8 + 8, 8), 8)
        h = pl.ds(pl.multiple_of(i * 8, 8), 8)
        cx = spread(tr[0, r, 0:128], tr[0, r, 128:256], hc[0, 0, h, :], hc[1, 0, h, :])
        cy = spread(tr[1, r, 0:128], tr[1, r, 128:256], hc[0, 1, h, :], hc[1, 1, h, :])
        cr = spread(re[r, 0:128], re[r, 128:256], hc[0, 2, h, :], hc[1, 2, h, :])
        live = [act[k, r, :].astype(F32) for k in range(4)]
        live.append(jnp.where(right, flip(live[0]), flip(live[3])))
        for kt in range(5):
            tx[kt, r, :] = cx[kt]
            ty[kt, r, :] = cy[kt]
            dg[kt, r, :] = cr[kt]
            ia[kt, r, :] = 1.0 - live[kt]
        return 0

    lax.fori_loop(0, SLABS, widen, 0, unroll=2)

    def diagonal(i, _):
        r = pl.ds(pl.multiple_of(i * 8 + 8, 8), 8)
        for kt in range(5):
            w = pltpu.roll(ty[kt, r, :], 1, 1)
            tyw[kt, r, :] = w
            d = dg[kt, r, :] + tx[kt, r, :] + tx[kt, pl.ds(i * 8 + 7, 8), :] + ty[kt, r, :] + w
            dg[kt, r, :] = d
            wd = OMEGA / jnp.maximum(d, 0.005)
            if kt < 4:
                wd = wd * (1.0 - ia[kt, r, :])
            for px in range(2):
                kd[px, kt, r, :] = wd
        return 0

    lax.fori_loop(0, SLABS, diagonal, 0, unroll=2)

    def keep(first, px):
        def body(i, _):
            r = pl.ds(pl.multiple_of(i * 8 + first, 8), 8)
            for k in range(4):
                kd[px, k, r, :] = kd[px, k, r, :] * sup[px, k, r, :].astype(F32)
            return 0

        return body

    lax.fori_loop(0, 29, keep(8, 0), 0, unroll=4)
    lax.fori_loop(0, 29, keep(48, 1), 0, unroll=4)

    arrived(sends)
    lax.fori_loop(0, 5, keep(240, 0), 0, unroll=5)
    lax.fori_loop(0, 5, keep(8, 1), 0, unroll=5)

    def unpack(i, _):
        r = pl.ds(pl.multiple_of(i * 8 + 8, 8), 8)
        live = 1.0 - ia[4, r, :]
        for px in range(2):
            yr = pl.ds(pl.multiple_of(i * 8 + (272 if px == 0 else 0), 8), 8)
            from_low, from_high = yl[0, yr, :], yl[1, yr, :]
            va[px, 4, r, :] = jnp.where(right, from_low, from_high)
            kept = flip(jnp.where(right, from_high, from_low)) * live
            kd[px, 4, r, :] = kd[px, 4, r, :] * kept
        return 0

    lax.fori_loop(0, SLABS, unpack, 0, unroll=17)

    def flux_sum(v, px, kt, i):
        r = pl.ds(pl.multiple_of(i * 8 + 8, 8), 8)
        mid = v[px, kt, r, :]
        up = v[px, kt, pl.ds(i * 8 + 9, 8), :]
        dn = v[px, kt, pl.ds(i * 8 + 7, 8), :]
        total = (
            tx[kt, r, :] * up
            + tx[kt, pl.ds(i * 8 + 7, 8), :] * dn
            + ty[kt, r, :] * pltpu.roll(mid, 127, 1)
            + tyw[kt, r, :] * pltpu.roll(mid, 1, 1)
        )
        return mid, total

    def sweep(src, dst):
        def first(i):
            r = pl.ds(pl.multiple_of(i * 8 + 8, 8), 8)
            raw = []
            for kt in range(5):
                for px in range(2):
                    mid, total = flux_sum(src, px, kt, i)
                    raw.append((1.0 - OMEGA) * mid + kd[px, kt, r, :] * total)
            turned = [flip(raw[2 * kt] + raw[2 * kt + 1]) for kt in range(5)]
            return tuple(raw), tuple(turned)

        def second(i, raw, turned):
            r = pl.ds(pl.multiple_of(i * 8 + 8, 8), 8)
            for kt in range(5):
                t = raw[2 * kt] + raw[2 * kt + 1]
                t = t + jnp.where(right, turned[(kt + 1) % 5], turned[(kt + 4) % 5])
                t = jnp.maximum(t + ia[kt, r, :], 1e-30)
                inv = pl.reciprocal(t, approx=True)
                inv = inv * (2.0 - t * inv)
                for px in range(2):
                    dst[px, kt, r, :] = raw[2 * kt + px] * inv

        def body(i, held):
            new = first(i)
            second(i - 1, *held)
            return new

        held = lax.fori_loop(1, SLABS, body, first(0), unroll=3)
        second(SLABS - 1, *held)

    sweep(va, vb)
    sweep(vb, va)
    sweep(va, vb)
    fin = vb

    def remote2(dx, dy, src, dst, i):
        return pltpu.make_async_remote_copy(
            src, dst, s2.at[i], r2.at[i], device_id=(gx + dx, gy + dy), device_id_type=MESH
        )

    backs = [
        ((-1, 0), remote2(-1, 0, fin.at[1, pl.ds(0, 4), pl.ds(16, 32), :], out.at[3, :, pl.ds(96, 32), :], 0)),
        ((1, 0), remote2(1, 0, fin.at[0, pl.ds(0, 4), pl.ds(240, 32), :], out.at[0, :, pl.ds(0, 32), :], 1)),
    ]
    for d, c in backs:
        start(d, [c])
    for side in range(2):
        def place_lanes(xs, side=side):
            m = None
            for g, x in enumerate(xs):
                x = roll(x, 32 * g if side == 0 else 32 * g + 32)
                m = x if m is None else jnp.where(lane < 32 * g, m, x)
            return m

        rs[side, 0:8, :] = place_lanes([fin[1, 4, 16 + 8 * g:24 + 8 * g, :] for g in range(4)])
        rs[side, 120:128, :] = place_lanes([fin[0, 4, 240 + 8 * g:248 + 8 * g, :] for g in range(4)])

        def pack_back(i, _, side=side, place_lanes=place_lanes):
            def at(px, first):
                return fin[px, 4, pl.ds(pl.multiple_of(first + i * 8, 8), 8), :]

            rs[side, pl.ds(pl.multiple_of(8 + i * 8, 8), 8), :] = place_lanes(
                [at(0, 16), at(0, 16 + 112), at(1, 48), at(1, 48 + 112)]
            )
            return 0

        lax.fori_loop(0, 14, pack_back, 0, unroll=14)

    for dx in (0, 1, -1):
        for dy, side in ((1, 0), (-1, 1)):
            at, n = {0: (8, 112), 1: (120, 8), -1: (0, 8)}[dx]
            i = 2 + {0: 0, 1: 1, -1: 2}[dx] * 2 + side
            backs.append(
                ((dx, dy), remote2(dx, dy, rs.at[side, pl.ds(at, n), :], rl.at[side, pl.ds(at, n), :], i))
            )
            start((dx, dy), [backs[-1][1]])

    def image(h, _):
        for kt in range(5):
            acc = [None] * 8
            for s in range(4):
                i = h * 4 + s + 1
                r = pl.ds(pl.multiple_of(i * 8 + 8, 8), 8)
                c = cls[kt, r, :]
                pick = [c == q for q in range(4)]
                for px in range(2):
                    mid, total = flux_sum(fin, px, kt, i)
                    img = dg[kt, r, :] * mid - total
                    for q in range(4):
                        n = (q // 2) * 4 + px * 2 + q % 2
                        x = jnp.where(pick[q], img, 0.0)
                        acc[n] = x if acc[n] is None else acc[n] + x
            zz[h, kt] = fold_rows(acc)
        return 0

    lax.fori_loop(0, 8, image, 0)

    table = jnp.zeros((8, 128), F32)
    bit_x, odd, bit_y = sub // 4, (sub // 2) % 2, sub % 2
    for a in range(5):
        part = jnp.zeros((8, 128), F32)
        base_x = a
        if a == 0:
            base_x = jnp.where(low_x, 1, 0)
        if a == 4:
            base_x = jnp.where(high_x, 3, 4)
        window_x = a - (a + odd) % 2
        dxo = window_x - (base_x - 1 + bit_x)
        for kt in range(5):
            z = zz[0, kt] if a == 0 else (zz[7, kt] if a == 4 else zz[2 * a - 1, kt] + zz[2 * a, kt])
            for shift in (32, 16, 8, 4, 2, 1):
                z = z + roll(z, -shift)
            for half in range(2):
                if kt < 4:
                    b, window_y = kt + half, kt
                else:
                    b, window_y = (4, 4) if half == 0 else (0, -1)
                base_y = b
                if b == 0:
                    base_y = jnp.where(low_y, 1, 0)
                if b == 4:
                    base_y = jnp.where(high_y, 3, 4)
                dyo = window_y - (base_y - 1 + bit_y)
                to = (base_y + bit_y) * 16 + (dxo + 1) * 3 + dyo + 1
                value = jnp.broadcast_to(z[:, 64 * half:64 * half + 1], (8, 128))
                part = part + jnp.where(lane == to, value, 0.0)
        low = jnp.sum(part[0:4], axis=0, keepdims=True)
        high = jnp.sum(part[4:8], axis=0, keepdims=True)
        table = table + jnp.where(sub == base_x, low, 0.0) + jnp.where(sub == base_x + 1, high, 0.0)
    tb[1, gx, 0:8, :] = table * (1.0 / 64.0)
    tb[1, gx, 8:16, :] = target

    hops = []
    for n, (s, t) in enumerate(peers):
        hops.append((t, pltpu.make_async_remote_copy(
            tb.at[1, gx], tb.at[1 - t, gx], st.at[n], rt.at[n],
            device_id=((gx + s) % NGX, gy + t), device_id_type=MESH,
        )))
    for t, c in hops:
        @pl.when(exists(0, t))
        def _(c=c):
            c.start()

    def emit(i, _):
        def one(j, px, first, to):
            for k in range(4):
                out[j, k, pl.ds(pl.multiple_of(to + i * 8, 8), 8), :] = fin[
                    px, k, pl.ds(pl.multiple_of(first + i * 8, 8), 8), :
                ]

        one(0, 0, 16, 32)
        one(1, 1, 48, 0)
        one(2, 0, 112, 0)
        one(3, 1, 176, 0)
        return 0

    lax.fori_loop(0, 12, emit, 0, unroll=4)
    for i in range(12, 16):
        for k in range(4):
            out[1, k, i * 8:i * 8 + 8, :] = fin[1, k, 48 + i * 8:56 + i * 8, :]
            out[2, k, i * 8:i * 8 + 8, :] = fin[0, k, 112 + i * 8:120 + i * 8, :]

    for (dx, dy), c in backs:
        @pl.when(exists(-dx, -dy))
        def _(c=c):
            c.wait_recv()

    for side, k in ((0, 0), (1, 3)):
        def merge(j, at, src, g):
            x = rl[side, pl.ds(src, 8), :]
            x = roll(x, -32 * g if side == 0 else 96 - 32 * g)
            inside = lane < 32 if side == 0 else lane >= 96
            out[j, k, at:at + 8, :] = jnp.where(inside, x, out[j, k, at:at + 8, :])

        for g in range(4):
            merge(0, 8 * g, 120, g)
            merge(3, 96 + 8 * g, 0, g)
        for s in range(28):
            j, at = (0, 32 + 8 * s) if s < 12 else (2, 8 * (s - 12))
            merge(j, at, 8 + 8 * (s % 14), s // 14)
            j, at = (1, 8 * s) if s < 16 else (3, 8 * (s - 16))
            merge(j, at, 8 + 8 * (s % 14), 2 + s // 14)

    for t, c in hops:
        @pl.when(exists(0, -t))
        def _(c=c):
            c.wait_recv()

    joined = []
    for s in range(NGX):
        a = tb[1, s, 0:8, :]
        below = roll(tb[0, s, 0:8, :], -64)
        above = roll(tb[2, s, 0:8, :], 64)
        group = lane // 16
        joined.append(a + jnp.where(group == 1, below, 0.0) + jnp.where(group == 4, above, 0.0))
    for s in range(NGX):
        t = joined[s]
        if s > 0:
            t = t + jnp.where(sub == 1, sroll(joined[s - 1], -4), 0.0)
        if s < NGX - 1:
            t = t + jnp.where(sub == 4, sroll(joined[s + 1], 4), 0.0)
        goal = tb[1, s, 8:16, :]
        for q in range(4):
            mine = jnp.where(goal == (gx * 4 + q).astype(F32), t, 0.0)
            line = jnp.sum(mine, axis=0, keepdims=True)
            line = line + pltpu.roll(line, 96, 1)
            line = line + pltpu.roll(line, 112, 1)
            rows_out[s * 4 + q:s * 4 + q + 1, :] = line[:, 16:25]

    for (dx, dy), cs in coef_sends + sends:
        @pl.when(exists(dx, dy))
        def _(cs=cs):
            for c in cs:
                c.wait_send()
    for (dx, dy), c in backs:
        @pl.when(exists(dx, dy))
        def _(c=c):
            c.wait_send()
    for t, c in hops:
        @pl.when(exists(0, t))
        def _(c=c):
            c.wait_send()


def local(basis, trans, reaction, support, codes, active, owner):
    anywhere = pl.BlockSpec(memory_space=pltpu.HBM)
    vmem = pl.BlockSpec(memory_space=pltpu.VMEM)
    sem = pltpu.SemaphoreType.DMA
    smoothed, coarse = pl.pallas_call(
        kernel,
        name="smooth",
        out_shape=(
            jax.ShapeDtypeStruct((4, 4, 128, 128), F32),
            jax.ShapeDtypeStruct((32, 9), F32),
        ),
        in_specs=[anywhere] * 6 + [pl.BlockSpec(memory_space=pltpu.SMEM)],
        out_specs=(vmem, vmem),
        scratch_shapes=[
            pltpu.VMEM((2, 5, ROWS, 128), F32),
            pltpu.VMEM((2, 5, ROWS, 128), F32),
            pltpu.VMEM((2, 4, ROWS, 128), jnp.int32),
            pltpu.VMEM((4, ROWS, 128), jnp.int32),
            pltpu.VMEM((4, ROWS, 128), jnp.int32),
            pltpu.VMEM((3, ROWS, 256), F32),
            pltpu.VMEM((ROWS, 256), F32),
            pltpu.VMEM((5, ROWS, 128), F32),
            pltpu.VMEM((5, ROWS, 128), F32),
            pltpu.VMEM((5, ROWS, 128), F32),
            pltpu.VMEM((5, ROWS, 128), F32),
            pltpu.VMEM((2, 5, ROWS, 128), F32),
            pltpu.VMEM((5, ROWS, 128), F32),
            pltpu.VMEM((2, 3, 272, 128), F32),
            pltpu.VMEM((2, 4, 40, 128), F32),
            pltpu.VMEM((2, 4, 40, 128), jnp.int32),
            pltpu.VMEM((2, YROWS, 128), F32),
            pltpu.VMEM((2, YROWS, 128), F32),
            pltpu.VMEM((2, CROWS, 128), F32),
            pltpu.VMEM((2, CROWS, 128), F32),
            pltpu.VMEM((2, 128, 128), F32),
            pltpu.VMEM((2, 128, 128), F32),
            pltpu.VMEM((3, NGX, 16, 128), F32),
            pltpu.VMEM((5, ROWS, 128), jnp.int32),
            pltpu.VMEM((8, 5, 8, 128), F32),
            sem((32,)), sem((24,)), sem((24,)), sem((8,)), sem((8,)), sem((24,)), sem((24,)),
        ],
        compiler_params=pltpu.CompilerParams(
            collective_id=0, has_side_effects=True, vmem_limit_bytes=60 << 20
        ),
    )(basis[0], trans[:, 0], reaction[0], support, codes, active[0], owner.reshape(16))
    return smoothed[None], coarse


def solution(mesh):
    return jax.shard_map(
        local,
        mesh=mesh,
        in_specs=(
            P(None, "gx", "gy", None, None),
            P(None, None, "gx", "gy"),
            P(None, "gx", "gy"),
            P("gx", "gy", None, None),
            P("gx", "gy", None, None),
            P(None, "gx", "gy", None, None),
            P(("gx", "gy"), None),
        ),
        out_specs=(P(None, "gx", "gy", None, None), P(("gx", "gy"), None)),
        check_vma=False,
    )
```

```python
import jax
import jax.numpy as jnp
from jax import lax
from jax.experimental import pallas as pl
from jax.experimental.pallas import tpu as pltpu
from jax.sharding import PartitionSpec as P

MESH = pl.DeviceIdType.MESH
OMEGA = 2.0 / 3.0
NGX, NGY = 8, 16
ROWS = 288
SLABS = 34
F32 = jnp.float32
YROWS = 392
CROWS = 64


def lanes():
    return lax.broadcasted_iota(jnp.int32, (8, 128), 1)


def subs():
    return lax.broadcasted_iota(jnp.int32, (8, 128), 0)


def roll(x, shift):
    shift = shift % 128
    return x if shift == 0 else pltpu.roll(x, shift, 1)


def sroll(x, shift):
    shift = shift % 8
    return x if shift == 0 else pltpu.roll(x, shift, 0)


def flip(x):
    return pltpu.roll(x, 64, 1)


def fold_rows(parts):
    sub = subs()
    step = 1
    while len(parts) > 1:
        low = (sub // step) % 2 == 0
        merged = []
        for i in range(0, len(parts), 2):
            a, b = parts[i], parts[i + 1]
            merged.append(jnp.where(low, a, sroll(b, step)) + jnp.where(low, sroll(a, -step), b))
        parts = merged
        step *= 2
    return parts[0]


def kernel(
    basis, trans, reaction, support, codes, active, owner,
    out, rows_out,
    va, vb, sup, act, cod, tr, re, tx, ty, tyw, dg, kd, ia, ds, dsup,
    ys, yl, yc, yd, rs, rl, tb, tg, cls, zz,
    lsem, ssem, rsem, s2, r2, st, rt, sg, rg,
):
    gx = lax.axis_index("gx")
    gy = lax.axis_index("gy")

    def exists(dx, dy):
        return (gx + dx >= 0) & (gx + dx < NGX) & (gy + dy >= 0) & (gy + dy < NGY)

    bar = pltpu.get_barrier_semaphore()
    peers = [(s, t) for t in (-1, 0, 1) for s in range(NGX) if (s, t) != (0, 0)]
    for s, t in peers:
        @pl.when(exists(0, t))
        def _(s=s, t=t):
            pl.semaphore_signal(bar, inc=1, device_id=((gx + s) % NGX, gy + t), device_id_type=MESH)

    loads = []

    def load(src, dst):
        c = pltpu.make_async_copy(src, dst, lsem.at[len(loads)])
        c.start()
        loads.append(c)

    load(trans, tr.at[:, pl.ds(16, 256), :])
    load(reaction, re.at[pl.ds(16, 256), :])
    n_coef = len(loads)
    wins = ((0, 24, 128, 0), (1, 0, 128, 1), (2, 0, 128, 0), (3, 0, 104, 1))
    for j, lo, hi, px in wins:
        at = 64 * j - 32 + lo + 16
        load(basis.at[j, :, pl.ds(lo, hi - lo), :], va.at[px, pl.ds(0, 4), pl.ds(at, hi - lo), :])
        load(support.at[j, :, pl.ds(lo, hi - lo), :], sup.at[px, :, pl.ds(at, hi - lo), :])
    for i, (j, lo) in enumerate(((0, 0), (3, 88))):
        load(basis.at[j, :, pl.ds(lo, 40), :], ds.at[i])
        load(support.at[j, :, pl.ds(lo, 40), :], dsup.at[i])
    n_first = len(loads)
    for j, lo, hi in ((0, 24, 128), (2, 0, 128), (3, 64, 104)):
        at = 64 * j - 32 + lo + 16
        load(active.at[j, :, pl.ds(lo, hi - lo), :], act.at[:, pl.ds(at, hi - lo), :])
        load(codes.at[j, :, pl.ds(lo, hi - lo), :], cod.at[:, pl.ds(at, hi - lo), :])

    zero = jnp.zeros((8, 128), F32)
    for buf in (va, vb):
        for px in range(2):
            for kt in range(5):
                buf[px, kt, 0:8, :] = zero
                buf[px, kt, 280:288, :] = zero
    for kt in range(5):
        tx[kt, 0:8, :] = zero

    for kt in range(4):
        va[1, kt, 8:12, :] = jnp.zeros((4, 128), F32)
        va[0, kt, 276:280, :] = jnp.zeros((4, 128), F32)
        sup[1, kt, 8:12, :] = jnp.zeros((4, 128), jnp.int32)
        sup[0, kt, 276:280, :] = jnp.zeros((4, 128), jnp.int32)
    for dx in (1, -1):
        @pl.when(jnp.logical_not(exists(-dx, 0)))
        def _(dx=dx):
            px, at, ring, j, lo = (1, 8, 8, 3, 0) if dx == 1 else (0, 240, 272, 0, 0)
            for kt in range(4):
                va[px, kt, at:at + 40, :] = jnp.zeros((40, 128), F32)
                sup[px, kt, at:at + 40, :] = jnp.zeros((40, 128), jnp.int32)
            for f in range(3):
                tr[f, ring:ring + 8, :] = jnp.zeros((8, 256), F32)
            re[ring:ring + 8, :] = jnp.zeros((8, 256), F32)
            jo, ro = (0, 0) if dx == 1 else (3, 96)
            for k in range(4):
                out[jo, k, ro:ro + 32, :] = jnp.zeros((32, 128), F32)
    for dy, side in ((1, 0), (-1, 1)):
        @pl.when(jnp.logical_not(exists(0, -dy)))
        def _(side=side, dy=dy):
            yl[side, 40:352, :] = jnp.zeros((312, 128), F32)
            yd[side, 8:56, :] = jnp.zeros((48, 128), F32)
            rl[side, 8:120, :] = jnp.zeros((112, 128), F32)
            for s in range(NGX):
                tb[1 - dy, s] = jnp.zeros((8, 128), F32)
        for dx in (1, -1):
            @pl.when(jnp.logical_not(exists(-dx, -dy)))
            def _(side=side, dx=dx):
                at = 0 if dx == 1 else 352
                yl[side, at:at + 40, :] = jnp.zeros((40, 128), F32)
                at = 0 if dx == 1 else 56
                yd[side, at:at + 8, :] = jnp.zeros((8, 128), F32)
                at = 120 if dx == 1 else 0
                rl[side, at:at + 8, :] = jnp.zeros((8, 128), F32)

    lane = lanes()
    sub = subs()
    right = lane >= 64

    for c in loads[:n_coef]:
        c.wait()

    def combine(i, _):
        r = pl.ds(pl.multiple_of(i * 8, 8), 8)
        re[r, :] = re[r, :] + tr[2, r, :]
        return 0

    lax.fori_loop(2, 34, combine, 0, unroll=8)

    def cells(f, at, high):
        col = slice(128, 256) if high else slice(0, 128)
        return tr[f, at:at + 8, col] if f < 2 else re[at:at + 8, col]

    for dy, side in ((1, 0), (-1, 1)):
        high = dy == 1
        for dx, at, to in ((1, 264, 0), (-1, 16, 56)):
            got = [roll(cells(f, at, high), (8 + 8 * f) if high else 8 * f) for f in range(3)]
            yc[side, to:to + 8, :] = jnp.where(lane < 8, got[0], jnp.where(lane < 16, got[1], got[2]))
        for f in range(3):
            for h in range(2):
                m = None
                for i in range(16):
                    x = roll(cells(f, 16 + h * 128 + i * 8, high), (8 * i + 8) if high else 8 * i)
                    m = x if m is None else jnp.where(lane < 8 * i, m, x)
                to = 8 + (f * 2 + h) * 8
                yc[side, to:to + 8, :] = m

    block = jnp.where(
        (sub >= 1) & (sub <= 4) & (lane >= 16) & (lane < 80), (sub - 1) * 4 + lane // 16 - 1, -1
    )
    own_of = jnp.full((8, 128), -1, jnp.int32)
    for n in range(16):
        own_of = jnp.where(block == n, owner[n], own_of)
    place = jnp.zeros((8, 128), jnp.int32)
    for n in range(16):
        place = place + jnp.where((own_of == owner[n]) & (block > n), 1, 0)
    tg[gx] = jnp.where(block >= 0, own_of * 4 + place, -1).astype(F32)

    for c in loads[n_coef:n_first]:
        c.wait()

    def chunks(xs, shift):
        m = None
        for n, x in enumerate(xs):
            x = roll(x, shift + 40 * n)
            m = x if m is None else jnp.where(lane < 40 * n, m, x)
        return m

    for dy, side, k, shift in ((1, 0, 3, -88), (-1, 1, 0, 0)):
        def value(i, px, k=k):
            return va[px, k, pl.ds(pl.multiple_of(i * 8 + (8 if px == 0 else 48), 8), 8), :]

        def mask(i, px, k=k):
            return sup[px, k, pl.ds(pl.multiple_of(i * 8 + (8 if px == 0 else 48), 8), 8), :].astype(F32)

        def pack(i, _, side=side, shift=shift, value=value, mask=mask):
            ys[side, pl.ds(pl.multiple_of(i * 8 + 40, 8), 8), :] = chunks(
                [value(i, 0), value(i, 1), mask(i, 0)], shift
            )
            return 0

        lax.fori_loop(0, 29, pack, 0, unroll=29)
        for i in range(10):
            ys[side, 272 + 8 * i:280 + 8 * i, :] = chunks(
                [mask(min(i + 10 * n, 28), 1) for n in range(3)], shift
            )
        for dx, jj in ((1, 1), (-1, 0)):
            base = 0 if dx == 1 else 352
            for n in range(5):
                b = ds[jj, k, n * 8:n * 8 + 8, :]
                p = flip(dsup[jj, k, n * 8:n * 8 + 8, :].astype(F32))
                ys[side, base + n * 8:base + n * 8 + 8, :] = (
                    jnp.where(right, b, p) if dy == 1 else jnp.where(right, p, b)
                )

    n_peers = 7 + NGX * (jnp.where(exists(0, -1), 1, 0) + jnp.where(exists(0, 1), 1, 0))
    pl.semaphore_wait(bar, n_peers)

    def remote(dx, dy, src, dst, i):
        return pltpu.make_async_remote_copy(
            src, dst, ssem.at[i], rsem.at[i], device_id=(gx + dx, gy + dy), device_id_type=MESH
        )

    def start(d, cs):
        @pl.when(exists(*d))
        def _():
            for c in cs:
                c.start()

    coef_sends, sends = [], []
    for dx in (1, -1):
        src, dst, i = (248, 8, 0) if dx == 1 else (0, 272, 2)
        coef_sends.append(((dx, 0), [
            remote(dx, 0, trans.at[:, pl.ds(src, 8), :], tr.at[:, pl.ds(dst, 8), :], i),
            remote(dx, 0, reaction.at[pl.ds(src, 8), :], re.at[pl.ds(dst, 8), :], i + 1),
        ]))
        start(*coef_sends[-1])
    for dx in (0, 1, -1):
        for dy, side in ((1, 0), (-1, 1)):
            at, n = {0: (8, 48), 1: (0, 8), -1: (56, 8)}[dx]
            i = 4 + {0: 0, 1: 1, -1: 2}[dx] * 2 + side
            coef_sends.append(((dx, dy), [
                remote(dx, dy, yc.at[side, pl.ds(at, n), :], yd.at[side, pl.ds(at, n), :], i)
            ]))
            start(*coef_sends[-1])
    def y_send(dx, dy, side):
        at, n = {0: (40, 312), 1: (0, 40), -1: (352, 40)}[dx]
        i = 14 + {0: 0, 1: 1, -1: 2}[dx] * 2 + side
        cs = [remote(dx, dy, ys.at[side, pl.ds(at, n), :], yl.at[side, pl.ds(at, n), :], i)]
        (sends if dx else side_sends).append(((dx, dy), cs))
        start((dx, dy), cs)

    side_sends = []
    y_send(0, 1, 0)
    y_send(0, -1, 1)
    for dx in (1, -1):
        j, lo, px, at, i = (3, 92, 1, 12, 10) if dx == 1 else (0, 0, 0, 240, 12)
        sends.append(((dx, 0), [
            remote(dx, 0, basis.at[j, :, pl.ds(lo, 36), :], va.at[px, pl.ds(0, 4), pl.ds(at, 36), :], i),
            remote(dx, 0, support.at[j, :, pl.ds(lo, 36), :], sup.at[px, :, pl.ds(at, 36), :], i + 1),
        ]))
        start(*sends[-1])
    for dx in (1, -1):
        y_send(dx, 1, 0)
        y_send(dx, -1, 1)
    goals = []
    for n in range(1, NGX):
        goals.append(pltpu.make_async_remote_copy(
            tg.at[gx], tg.at[gx], sg.at[n], rg.at[n],
            device_id=((gx + n) % NGX, gy), device_id_type=MESH,
        ))

    for c in loads[n_first:]:
        c.wait()

    low_x, high_x = gx == 0, gx == NGX - 1
    low_y, high_y = gy == 0, gy == NGY - 1

    def classify(i, _):
        r = pl.ds(pl.multiple_of(i * 8 + 16, 8), 8)
        h = i // 4
        thx = jnp.where((h == 0) | (h == 3) | (h == 4), 3, 6)
        thx = jnp.where((h == 0) & low_x, 6, thx)
        thx = jnp.where((h == 7) & high_x, 3, thx)
        got = []
        for k in range(4):
            c = cod[k, r, :]
            cy = c - 3 * (jnp.where(c >= 3, 1, 0) + jnp.where(c >= 6, 1, 0))
            thl = jnp.where(low_y, 2, 1) if k == 0 else 1
            thr = jnp.where(high_y, 1, 2) if k == 3 else 2
            thy = jnp.where(right, thr, thl)
            v = jnp.where(c >= thx, 2, 0) + jnp.where(cy >= thy, 1, 0)
            got.append(jnp.where(act[k, r, :] > 0, v, 4))
        k4 = jnp.where(right, flip(got[0]), flip(got[3]))
        cls[0, r, :] = jnp.where(lane >= 32, got[0], 4)
        cls[1, r, :] = got[1]
        cls[2, r, :] = got[2]
        cls[3, r, :] = jnp.where(lane < 96, got[3], 4)
        cls[4, r, :] = jnp.where((lane < 32) | (lane >= 96), k4, 4)
        return 0

    lax.fori_loop(0, 32, classify, 0, unroll=4)

    def arrived(copies):
        for (dx, dy), cs in copies:
            @pl.when(exists(-dx, -dy))
            def _(cs=cs):
                for c in cs:
                    c.wait_recv()

    def spread(t0, t1):
        r0, l0, r1, l1 = roll(t0, 32), roll(t0, -32), roll(t1, 32), roll(t1, -32)
        k0 = jnp.where(lane < 32, 0.0, r0)
        k1 = jnp.where(lane < 96, l0, l1)
        k2 = jnp.where(lane < 32, r0, r1)
        k3 = jnp.where(lane < 96, l1, 0.0)
        return [k0, k1, k2, k3, jnp.where(right, flip(k0), flip(k3))]

    def widen(i, _):
        r = pl.ds(pl.multiple_of(i * 8 + 8, 8), 8)
        cx = spread(tr[0, r, 0:128], tr[0, r, 128:256])
        cy = spread(tr[1, r, 0:128], tr[1, r, 128:256])
        cr = spread(re[r, 0:128], re[r, 128:256])
        for kt in range(5):
            tx[kt, r, :] = cx[kt]
            ty[kt, r, :] = cy[kt]
            dg[kt, r, :] = cr[kt]
        return 0

    def dead(i, _):
        r = pl.ds(pl.multiple_of(i * 8 + 8, 8), 8)
        live = [act[k, r, :].astype(F32) for k in range(4)]
        live.append(jnp.where(right, flip(live[0]), flip(live[3])))
        for kt in range(5):
            ia[kt, r, :] = 1.0 - live[kt]
        return 0

    def diagonal(lo, hi, kts, unroll):
        own = (lo < 29, lo >= 5)

        def body(i, _):
            r = pl.ds(pl.multiple_of(i * 8 + 8, 8), 8)
            for kt in kts:
                w = pltpu.roll(ty[kt, r, :], 1, 1)
                tyw[kt, r, :] = w
                d = dg[kt, r, :] + tx[kt, r, :] + tx[kt, pl.ds(i * 8 + 7, 8), :] + ty[kt, r, :] + w
                dg[kt, r, :] = d
                inv = pl.reciprocal(jnp.maximum(d, 0.005), approx=True)
                inv = inv * (2.0 - jnp.maximum(d, 0.005) * inv)
                wd = (OMEGA * inv) * (1.0 - ia[kt, r, :])
                for px in range(2):
                    if kt < 4 and own[px]:
                        kd[px, kt, r, :] = wd * sup[px, kt, r, :].astype(F32)
                    else:
                        kd[px, kt, r, :] = wd
            return 0

        lax.fori_loop(lo, hi, body, 0, unroll=unroll)

    lax.fori_loop(1, 33, widen, 0, unroll=2)
    lax.fori_loop(0, SLABS, dead, 0, unroll=2)
    diagonal(2, 5, (1, 2), 3)
    diagonal(5, 29, (1, 2), 4)
    diagonal(29, 33, (1, 2), 4)

    arrived(coef_sends)
    for c in goals:
        c.start()
    for at in (8, 272):
        re[at:at + 8, :] = re[at:at + 8, :] + tr[2, at:at + 8, :]
    widen(0, 0)
    widen(33, 0)
    for f, ref in enumerate((tx, ty, dg)):
        for n in range(SLABS):
            if n == 0 or n == SLABS - 1:
                at, away = (0 if n == 0 else 56), 8 * f
            else:
                h, i = divmod(n - 1, 16)
                at, away = 8 + (f * 2 + h) * 8, 8 * i
            x0, x1 = yd[0, at:at + 8, :], yd[1, at:at + 8, :]
            r = slice(8 * n + 8, 8 * n + 16)
            ref[0, r, :] = jnp.where((lane >= 24) & (lane < 32), roll(x0, 24 - away), ref[0, r, :])
            ref[3, r, :] = jnp.where((lane >= 96) & (lane < 104), roll(x1, 96 - away), ref[3, r, :])
            x = jnp.where((lane >= 88) & (lane < 96), roll(x0, 88 - away), ref[4, r, :])
            ref[4, r, :] = jnp.where((lane >= 32) & (lane < 40), roll(x1, 32 - away), x)
    diagonal(0, 2, (1, 2), 2)
    diagonal(33, 34, (1, 2), 1)
    diagonal(0, 5, (0, 3, 4), 5)
    diagonal(5, 29, (0, 3, 4), 4)
    diagonal(29, 34, (0, 3, 4), 5)

    def keep(first, px):
        def body(i, _):
            r = pl.ds(pl.multiple_of(i * 8 + first, 8), 8)
            for k in range(4):
                kd[px, k, r, :] = kd[px, k, r, :] * sup[px, k, r, :].astype(F32)
            return 0

        return body

    def flux_sum(v, px, kt, i):
        r = pl.ds(pl.multiple_of(i * 8 + 8, 8), 8)
        mid = v[px, kt, r, :]
        up = v[px, kt, pl.ds(i * 8 + 9, 8), :]
        dn = v[px, kt, pl.ds(i * 8 + 7, 8), :]
        total = (
            tx[kt, r, :] * up
            + tx[kt, pl.ds(i * 8 + 7, 8), :] * dn
            + ty[kt, r, :] * pltpu.roll(mid, 127, 1)
            + tyw[kt, r, :] * pltpu.roll(mid, 1, 1)
        )
        return mid, total

    def sweep(src, dst, starts, count, unroll):
        def first(i):
            r = pl.ds(pl.multiple_of(i * 8 + 8, 8), 8)
            raw = []
            for kt in range(5):
                for px in range(2):
                    mid, total = flux_sum(src, px, kt, i)
                    raw.append((1.0 - OMEGA) * mid + kd[px, kt, r, :] * total)
            turned = [flip(raw[2 * kt] + raw[2 * kt + 1]) for kt in range(5)]
            return tuple(raw), tuple(turned)

        def second(i, raw, turned):
            r = pl.ds(pl.multiple_of(i * 8 + 8, 8), 8)
            for kt in range(5):
                t = raw[2 * kt] + raw[2 * kt + 1]
                t = t + jnp.where(right, turned[(kt + 1) % 5], turned[(kt + 4) % 5])
                t = jnp.maximum(t + ia[kt, r, :], 1e-30)
                inv = pl.reciprocal(t, approx=True)
                inv = inv * (2.0 - t * inv)
                for px in range(2):
                    dst[px, kt, r, :] = raw[2 * kt + px] * inv

        def firsts(i):
            return tuple(first(n + i) for n in starts)

        def body(i, held):
            new = firsts(i)
            for n, h in zip(starts, held):
                second(n + i - 1, *h)
            return new

        held = lax.fori_loop(1, count, body, firsts(0), unroll=unroll)
        for n, h in zip(starts, held):
            second(n + count - 1, *h)

    fin = vb

    def image(h, _):
        for kt in range(5):
            acc = [None] * 8
            for s in range(4):
                i = h * 4 + s + 1
                r = pl.ds(pl.multiple_of(i * 8 + 8, 8), 8)
                c = cls[kt, r, :]
                pick = [c == q for q in range(4)]
                for px in range(2):
                    mid, total = flux_sum(fin, px, kt, i)
                    img = dg[kt, r, :] * mid - total
                    for q in range(4):
                        n = (q // 2) * 4 + px * 2 + q % 2
                        x = jnp.where(pick[q], img, 0.0)
                        acc[n] = x if acc[n] is None else acc[n] + x
            zz[h, kt] = fold_rows(acc)
        return 0


    def remote2(dx, dy, src, dst, i):
        return pltpu.make_async_remote_copy(
            src, dst, s2.at[i], r2.at[i], device_id=(gx + dx, gy + dy), device_id_type=MESH
        )

    late = ((1, 2, 3, 4, 5, 6, 7, 26, 27, 28), (5, 6, 7, 26, 27, 28, 29, 30, 31, 32))
    backs = []

    def put(side, at, places):
        m = None
        for g, (px, n) in enumerate(places):
            x = roll(fin[px, 4, 8 * n + 8:8 * n + 16, :], 32 * g if side == 0 else 32 * g + 32)
            m = x if m is None else jnp.where(lane < 32 * g, m, x)
        rs[side, at:at + 8, :] = m

    def back(dx, dy, src, dst, i):
        backs.append(((dx, dy), remote2(dx, dy, src, dst, i)))
        start((dx, dy), [backs[-1][1]])

    def back_side(dx, at, n, i):
        for dy, side in ((1, 0), (-1, 1)):
            back(dx, dy, rs.at[side, pl.ds(at, n), :], rl.at[side, pl.ds(at, n), :], i + side)

    early_places = [[(0, 8 + m), (0, 17 + m), (1, 8 + m), (1, 17 + m)] for m in range(9)]
    late_places = [[(0, late[0][m]), (0, late[0][m + 5]), (1, late[1][m]), (1, late[1][m + 5])] for m in range(5)]

    arrived(side_sends)

    def apart(m0, m1, n):
        return jnp.where(
            lane < 40, roll(m1, -40 * n), jnp.where(lane >= 88, roll(m0, 88 - 40 * n), 0.0)
        )

    def unpack(i, _):
        yr = pl.ds(pl.multiple_of(i * 8 + 40, 8), 8)
        even = pl.ds(pl.multiple_of(i * 8 + 8, 8), 8)
        odd = pl.ds(pl.multiple_of(i * 8 + 48, 8), 8)
        m0, m1 = yl[0, yr, :], yl[1, yr, :]
        va[0, 4, even, :] = apart(m0, m1, 0)
        va[1, 4, odd, :] = apart(m0, m1, 1)
        kd[0, 4, even, :] = kd[0, 4, even, :] * apart(m0, m1, 2)
        return 0

    lax.fori_loop(0, 29, unpack, 0, unroll=8)
    for i in range(10):
        m0, m1 = yl[0, 272 + 8 * i:280 + 8 * i, :], yl[1, 272 + 8 * i:280 + 8 * i, :]
        for n in range(3):
            at = 48 + 8 * (i + 10 * n)
            if i + 10 * n < 29:
                kd[1, 4, at:at + 8, :] = kd[1, 4, at:at + 8, :] * apart(m0, m1, n)

    sweep(va, vb, (6,), 22, 3)
    sweep(vb, va, (7,), 20, 3)
    sweep(va, vb, (8,), 18, 3)
    for side in range(2):
        for m in range(9):
            put(side, 8 + 8 * m, early_places[m])
    back_side(0, 8, 72, 0)
    lax.fori_loop(2, 6, image, 0)

    arrived(sends)
    lax.fori_loop(0, 5, keep(240, 0), 0, unroll=5)
    lax.fori_loop(0, 5, keep(8, 1), 0, unroll=5)
    for px, at, to in ((1, 0, 8), (0, 352, 240)):
        for n in range(5):
            m0, m1 = yl[0, at + 8 * n:at + 8 * n + 8, :], yl[1, at + 8 * n:at + 8 * n + 8, :]
            r = slice(to + 8 * n, to + 8 * n + 8)
            va[px, 4, r, :] = jnp.where(right, m0, m1)
            kd[px, 4, r, :] = kd[px, 4, r, :] * flip(jnp.where(right, m1, m0))

    sweep(va, vb, (0, 28), 6, 2)
    sweep(vb, va, (0, 27), 7, 2)
    sweep(va, vb, (0, 26), 8, 2)

    back(-1, 0, fin.at[1, pl.ds(0, 4), pl.ds(16, 32), :], out.at[3, :, pl.ds(96, 32), :], 2)
    back(1, 0, fin.at[0, pl.ds(0, 4), pl.ds(240, 32), :], out.at[0, :, pl.ds(0, 32), :], 3)
    for side in range(2):
        for m in range(5):
            put(side, 80 + 8 * m, late_places[m])
        put(side, 0, [(1, n) for n in range(1, 5)])
        put(side, 120, [(0, n) for n in range(29, 33)])
    back_side(0, 80, 40, 4)
    back_side(1, 120, 8, 6)
    back_side(-1, 0, 8, 8)

    lax.fori_loop(0, 2, image, 0)
    lax.fori_loop(6, 8, image, 0)

    table = jnp.zeros((8, 128), F32)
    bit_x, odd, bit_y = sub // 4, (sub // 2) % 2, sub % 2
    for a in range(5):
        part = jnp.zeros((8, 128), F32)
        base_x = a
        if a == 0:
            base_x = jnp.where(low_x, 1, 0)
        if a == 4:
            base_x = jnp.where(high_x, 3, 4)
        window_x = a - (a + odd) % 2
        dxo = window_x - (base_x - 1 + bit_x)
        for kt in range(5):
            z = zz[0, kt] if a == 0 else (zz[7, kt] if a == 4 else zz[2 * a - 1, kt] + zz[2 * a, kt])
            for shift in (32, 16, 8, 4, 2, 1):
                z = z + roll(z, -shift)
            for half in range(2):
                if kt < 4:
                    b, window_y = kt + half, kt
                else:
                    b, window_y = (4, 4) if half == 0 else (0, -1)
                base_y = b
                if b == 0:
                    base_y = jnp.where(low_y, 1, 0)
                if b == 4:
                    base_y = jnp.where(high_y, 3, 4)
                dyo = window_y - (base_y - 1 + bit_y)
                to = (base_y + bit_y) * 16 + (dxo + 1) * 3 + dyo + 1
                value = jnp.broadcast_to(z[:, 64 * half:64 * half + 1], (8, 128))
                part = part + jnp.where(lane == to, value, 0.0)
        low = jnp.sum(part[0:4], axis=0, keepdims=True)
        high = jnp.sum(part[4:8], axis=0, keepdims=True)
        table = table + jnp.where(sub == base_x, low, 0.0) + jnp.where(sub == base_x + 1, high, 0.0)
    tb[1, gx] = table * (1.0 / 64.0)

    hops = []
    for n, (s, t) in enumerate(peers):
        hops.append((t, pltpu.make_async_remote_copy(
            tb.at[1, gx], tb.at[1 - t, gx], st.at[n], rt.at[n],
            device_id=((gx + s) % NGX, gy + t), device_id_type=MESH,
        )))
    for t, c in hops:
        @pl.when(exists(0, t))
        def _(c=c):
            c.start()

    def emit(i, _):
        def one(j, px, first, to):
            for k in range(4):
                out[j, k, pl.ds(pl.multiple_of(to + i * 8, 8), 8), :] = fin[
                    px, k, pl.ds(pl.multiple_of(first + i * 8, 8), 8), :
                ]

        one(0, 0, 16, 32)
        one(1, 1, 48, 0)
        one(2, 0, 112, 0)
        one(3, 1, 176, 0)
        return 0

    lax.fori_loop(0, 12, emit, 0, unroll=4)
    for i in range(12, 16):
        for k in range(4):
            out[1, k, i * 8:i * 8 + 8, :] = fin[1, k, 48 + i * 8:56 + i * 8, :]
            out[2, k, i * 8:i * 8 + 8, :] = fin[0, k, 112 + i * 8:120 + i * 8, :]

    for (dx, dy), c in backs:
        @pl.when(exists(-dx, -dy))
        def _(c=c):
            c.wait_recv()

    for side, k in ((0, 0), (1, 3)):
        def merge(j, at, src, g):
            x = rl[side, pl.ds(src, 8), :]
            x = roll(x, -32 * g if side == 0 else 96 - 32 * g)
            inside = lane < 32 if side == 0 else lane >= 96
            out[j, k, at:at + 8, :] = jnp.where(inside, x, out[j, k, at:at + 8, :])

        for g in range(4):
            merge(0, 8 * g, 120, g)
            merge(3, 96 + 8 * g, 0, g)
        for first, places in ((8, early_places), (80, late_places)):
            for m, four in enumerate(places):
                for g, (px, n) in enumerate(four):
                    row = 8 * (n - 1)
                    if px == 0:
                        j, at = (0, row + 32) if row < 96 else (2, row - 96)
                    else:
                        j, at = (1, row - 32) if row < 160 else (3, row - 160)
                    merge(j, at, first + 8 * m, g)

    for t, c in hops:
        @pl.when(exists(0, -t))
        def _(c=c):
            c.wait_recv()

    for c in goals:
        c.wait_recv()

    joined = []
    for s in range(NGX):
        a = tb[1, s]
        below = roll(tb[0, s], -64)
        above = roll(tb[2, s], 64)
        group = lane // 16
        joined.append(a + jnp.where(group == 1, below, 0.0) + jnp.where(group == 4, above, 0.0))
    for s in range(NGX):
        t = joined[s]
        if s > 0:
            t = t + jnp.where(sub == 1, sroll(joined[s - 1], -4), 0.0)
        if s < NGX - 1:
            t = t + jnp.where(sub == 4, sroll(joined[s + 1], 4), 0.0)
        goal = tg[s]
        for q in range(4):
            mine = jnp.where(goal == (gx * 4 + q).astype(F32), t, 0.0)
            line = jnp.sum(mine, axis=0, keepdims=True)
            line = line + pltpu.roll(line, 96, 1)
            line = line + pltpu.roll(line, 112, 1)
            rows_out[s * 4 + q:s * 4 + q + 1, :] = line[:, 16:25]

    for (dx, dy), cs in coef_sends + side_sends + sends:
        @pl.when(exists(dx, dy))
        def _(cs=cs):
            for c in cs:
                c.wait_send()
    for (dx, dy), c in backs:
        @pl.when(exists(dx, dy))
        def _(c=c):
            c.wait_send()
    for t, c in hops:
        @pl.when(exists(0, t))
        def _(c=c):
            c.wait_send()
    for c in goals:
        c.wait_send()


def local(basis, trans, reaction, support, codes, active, owner):
    anywhere = pl.BlockSpec(memory_space=pltpu.HBM)
    vmem = pl.BlockSpec(memory_space=pltpu.VMEM)
    sem = pltpu.SemaphoreType.DMA
    smoothed, coarse = pl.pallas_call(
        kernel,
        name="smooth",
        out_shape=(
            pltpu.VMEM((4, 4, 128, 128), F32),
            pltpu.VMEM((32, 9), F32),
        ),
        in_specs=[anywhere] * 6 + [pl.BlockSpec(memory_space=pltpu.SMEM)],
        out_specs=(vmem, vmem),
        scratch_shapes=[
            pltpu.VMEM((2, 5, ROWS, 128), F32),
            pltpu.VMEM((2, 5, ROWS, 128), F32),
            pltpu.VMEM((2, 4, ROWS, 128), jnp.int32),
            pltpu.VMEM((4, ROWS, 128), jnp.int32),
            pltpu.VMEM((4, ROWS, 128), jnp.int32),
            pltpu.VMEM((3, ROWS, 256), F32),
            pltpu.VMEM((ROWS, 256), F32),
            pltpu.VMEM((5, ROWS, 128), F32),
            pltpu.VMEM((5, ROWS, 128), F32),
            pltpu.VMEM((5, ROWS, 128), F32),
            pltpu.VMEM((5, ROWS, 128), F32),
            pltpu.VMEM((2, 5, ROWS, 128), F32),
            pltpu.VMEM((5, ROWS, 128), F32),
            pltpu.VMEM((2, 4, 40, 128), F32),
            pltpu.VMEM((2, 4, 40, 128), jnp.int32),
            pltpu.VMEM((2, YROWS, 128), F32),
            pltpu.VMEM((2, YROWS, 128), F32),
            pltpu.VMEM((2, CROWS, 128), F32),
            pltpu.VMEM((2, CROWS, 128), F32),
            pltpu.VMEM((2, 128, 128), F32),
            pltpu.VMEM((2, 128, 128), F32),
            pltpu.VMEM((3, NGX, 8, 128), F32),
            pltpu.VMEM((NGX, 8, 128), F32),
            pltpu.VMEM((5, ROWS, 128), jnp.int32),
            pltpu.VMEM((8, 5, 8, 128), F32),
            sem((32,)), sem((24,)), sem((24,)), sem((10,)), sem((10,)), sem((24,)), sem((24,)), sem((8,)), sem((8,)),
        ],
        compiler_params=pltpu.CompilerParams(
            collective_id=0, has_side_effects=True, vmem_limit_bytes=60 << 20
        ),
    )(basis[0], trans[:, 0], reaction[0], support, codes, active[0], owner.reshape(16))
    return smoothed[None], coarse


def solution(mesh):
    return jax.shard_map(
        local,
        mesh=mesh,
        in_specs=(
            P(None, "gx", "gy", None, None),
            P(None, None, "gx", "gy"),
            P(None, "gx", "gy"),
            P("gx", "gy", None, None),
            P("gx", "gy", None, None),
            P(None, "gx", "gy", None, None),
            P(("gx", "gy"), None),
        ),
        out_specs=(P(None, "gx", "gy", None, None), P(("gx", "gy"), None)),
        check_vma=False,
    )
```

```python
import jax
import jax.numpy as jnp
from jax import lax
from jax.experimental import pallas as pl
from jax.experimental.pallas import tpu as pltpu
from jax.sharding import PartitionSpec as P

MESH = pl.DeviceIdType.MESH
OMEGA = 2.0 / 3.0
NGX, NGY = 8, 16
ROWS = 288
SLABS = 34
F32 = jnp.float32
YROWS = 392
CROWS = 64


def lanes():
    return lax.broadcasted_iota(jnp.int32, (8, 128), 1)


def subs():
    return lax.broadcasted_iota(jnp.int32, (8, 128), 0)


def roll(x, shift):
    shift = shift % 128
    return x if shift == 0 else pltpu.roll(x, shift, 1)


def sroll(x, shift):
    shift = shift % 8
    return x if shift == 0 else pltpu.roll(x, shift, 0)


def flip(x):
    return pltpu.roll(x, 64, 1)


def fold_rows(parts):
    sub = subs()
    step = 1
    while len(parts) > 1:
        low = (sub // step) % 2 == 0
        merged = []
        for i in range(0, len(parts), 2):
            a, b = parts[i], parts[i + 1]
            merged.append(jnp.where(low, a, sroll(b, step)) + jnp.where(low, sroll(a, -step), b))
        parts = merged
        step *= 2
    return parts[0]


def kernel(
    basis, trans, reaction, support, codes, active, owner,
    out, rows_out,
    va, vb, sup, act, cod, tr, re, tx, ty, tyw, dg, kd, ia, ds, dsup,
    ys, yl, yc, yd, rs, rl, tb, tg, cls, zz,
    lsem, ssem, rsem, s2, r2, st, rt, sg, rg,
):
    gx = lax.axis_index("gx")
    gy = lax.axis_index("gy")

    def exists(dx, dy):
        return (gx + dx >= 0) & (gx + dx < NGX) & (gy + dy >= 0) & (gy + dy < NGY)

    bar = pltpu.get_barrier_semaphore()
    peers = [(s, t) for t in (-1, 0, 1) for s in range(NGX) if (s, t) != (0, 0)]
    for s, t in peers:
        @pl.when(exists(0, t))
        def _(s=s, t=t):
            pl.semaphore_signal(bar, inc=1, device_id=((gx + s) % NGX, gy + t), device_id_type=MESH)

    loads = []

    def load(src, dst):
        c = pltpu.make_async_copy(src, dst, lsem.at[len(loads)])
        c.start()
        loads.append(c)

    load(trans, tr.at[:, pl.ds(16, 256), :])
    load(reaction, re.at[pl.ds(16, 256), :])
    n_coef = len(loads)
    wins = ((0, 24, 128, 0), (1, 0, 128, 1), (2, 0, 128, 0), (3, 0, 104, 1))
    for j, lo, hi, px in wins:
        at = 64 * j - 32 + lo + 16
        load(basis.at[j, :, pl.ds(lo, hi - lo), :], va.at[px, pl.ds(0, 4), pl.ds(at, hi - lo), :])
        load(support.at[j, :, pl.ds(lo, hi - lo), :], sup.at[px, :, pl.ds(at, hi - lo), :])
    for i, (j, lo) in enumerate(((0, 0), (3, 88))):
        load(basis.at[j, :, pl.ds(lo, 40), :], ds.at[i])
        load(support.at[j, :, pl.ds(lo, 40), :], dsup.at[i])
    n_first = len(loads)
    for j, lo, hi in ((0, 24, 128), (2, 0, 128), (3, 64, 104)):
        at = 64 * j - 32 + lo + 16
        load(active.at[j, :, pl.ds(lo, hi - lo), :], act.at[:, pl.ds(at, hi - lo), :])
        load(codes.at[j, :, pl.ds(lo, hi - lo), :], cod.at[:, pl.ds(at, hi - lo), :])

    zero = jnp.zeros((8, 128), F32)
    for buf in (va, vb):
        for px in range(2):
            for kt in range(5):
                buf[px, kt, 0:8, :] = zero
                buf[px, kt, 280:288, :] = zero
    for kt in range(5):
        tx[kt, 0:8, :] = zero

    for kt in range(4):
        va[1, kt, 8:12, :] = jnp.zeros((4, 128), F32)
        va[0, kt, 276:280, :] = jnp.zeros((4, 128), F32)
        sup[1, kt, 8:12, :] = jnp.zeros((4, 128), jnp.int32)
        sup[0, kt, 276:280, :] = jnp.zeros((4, 128), jnp.int32)
    for dx in (1, -1):
        @pl.when(jnp.logical_not(exists(-dx, 0)))
        def _(dx=dx):
            px, at, ring, j, lo = (1, 8, 8, 3, 0) if dx == 1 else (0, 240, 272, 0, 0)
            for kt in range(4):
                va[px, kt, at:at + 40, :] = jnp.zeros((40, 128), F32)
                sup[px, kt, at:at + 40, :] = jnp.zeros((40, 128), jnp.int32)
            for f in range(3):
                tr[f, ring:ring + 8, :] = jnp.zeros((8, 256), F32)
            re[ring:ring + 8, :] = jnp.zeros((8, 256), F32)
            jo, ro = (0, 0) if dx == 1 else (3, 96)
            for k in range(4):
                out[jo, k, ro:ro + 32, :] = jnp.zeros((32, 128), F32)
    for dy, side in ((1, 0), (-1, 1)):
        @pl.when(jnp.logical_not(exists(0, -dy)))
        def _(side=side, dy=dy):
            yl[side, 40:352, :] = jnp.zeros((312, 128), F32)
            yd[side, 8:56, :] = jnp.zeros((48, 128), F32)
            rl[side, 8:120, :] = jnp.zeros((112, 128), F32)
            for s in range(NGX):
                tb[1 - dy, s] = jnp.zeros((8, 128), F32)
        for dx in (1, -1):
            @pl.when(jnp.logical_not(exists(-dx, -dy)))
            def _(side=side, dx=dx):
                at = 0 if dx == 1 else 352
                yl[side, at:at + 40, :] = jnp.zeros((40, 128), F32)
                at = 0 if dx == 1 else 56
                yd[side, at:at + 8, :] = jnp.zeros((8, 128), F32)
                at = 120 if dx == 1 else 0
                rl[side, at:at + 8, :] = jnp.zeros((8, 128), F32)

    lane = lanes()
    sub = subs()
    right = lane >= 64

    for c in loads[:n_coef]:
        c.wait()

    def combine(i, _):
        r = pl.ds(pl.multiple_of(i * 8, 8), 8)
        re[r, :] = re[r, :] + tr[2, r, :]
        return 0

    lax.fori_loop(2, 34, combine, 0, unroll=8)

    def cells(f, at, high):
        col = slice(128, 256) if high else slice(0, 128)
        return tr[f, at:at + 8, col] if f < 2 else re[at:at + 8, col]

    for dy, side in ((1, 0), (-1, 1)):
        high = dy == 1
        for dx, at, to in ((1, 264, 0), (-1, 16, 56)):
            got = [roll(cells(f, at, high), (8 + 8 * f) if high else 8 * f) for f in range(3)]
            yc[side, to:to + 8, :] = jnp.where(lane < 8, got[0], jnp.where(lane < 16, got[1], got[2]))
        for f in range(3):
            for h in range(2):
                m = None
                for i in range(16):
                    x = roll(cells(f, 16 + h * 128 + i * 8, high), (8 * i + 8) if high else 8 * i)
                    m = x if m is None else jnp.where(lane < 8 * i, m, x)
                to = 8 + (f * 2 + h) * 8
                yc[side, to:to + 8, :] = m

    block = jnp.where(
        (sub >= 1) & (sub <= 4) & (lane >= 16) & (lane < 80), (sub - 1) * 4 + lane // 16 - 1, -1
    )
    own_of = jnp.full((8, 128), -1, jnp.int32)
    for n in range(16):
        own_of = jnp.where(block == n, owner[n], own_of)
    place = jnp.zeros((8, 128), jnp.int32)
    for n in range(16):
        place = place + jnp.where((own_of == owner[n]) & (block > n), 1, 0)
    tg[gx] = jnp.where(block >= 0, own_of * 4 + place, -1).astype(F32)

    for c in loads[n_coef:n_first]:
        c.wait()

    def chunks(xs, shift):
        m = None
        for n, x in enumerate(xs):
            x = roll(x, shift + 40 * n)
            m = x if m is None else jnp.where(lane < 40 * n, m, x)
        return m

    for dy, side, k, shift in ((1, 0, 3, -88), (-1, 1, 0, 0)):
        def value(i, px, k=k):
            return va[px, k, pl.ds(pl.multiple_of(i * 8 + (8 if px == 0 else 48), 8), 8), :]

        def mask(i, px, k=k):
            return sup[px, k, pl.ds(pl.multiple_of(i * 8 + (8 if px == 0 else 48), 8), 8), :].astype(F32)

        def pack(i, _, side=side, shift=shift, value=value, mask=mask):
            ys[side, pl.ds(pl.multiple_of(i * 8 + 40, 8), 8), :] = chunks(
                [value(i, 0), value(i, 1), mask(i, 0)], shift
            )
            return 0

        lax.fori_loop(0, 29, pack, 0, unroll=29)
        for i in range(10):
            ys[side, 272 + 8 * i:280 + 8 * i, :] = chunks(
                [mask(min(i + 10 * n, 28), 1) for n in range(3)], shift
            )
        for dx, jj in ((1, 1), (-1, 0)):
            base = 0 if dx == 1 else 352
            for n in range(5):
                b = ds[jj, k, n * 8:n * 8 + 8, :]
                p = flip(dsup[jj, k, n * 8:n * 8 + 8, :].astype(F32))
                ys[side, base + n * 8:base + n * 8 + 8, :] = (
                    jnp.where(right, b, p) if dy == 1 else jnp.where(right, p, b)
                )

    n_peers = 7 + NGX * (jnp.where(exists(0, -1), 1, 0) + jnp.where(exists(0, 1), 1, 0))
    pl.semaphore_wait(bar, n_peers)

    def remote(dx, dy, src, dst, i):
        return pltpu.make_async_remote_copy(
            src, dst, ssem.at[i], rsem.at[i], device_id=(gx + dx, gy + dy), device_id_type=MESH
        )

    def start(d, cs):
        @pl.when(exists(*d))
        def _():
            for c in cs:
                c.start()

    coef_sends, sends = [], []
    for dx in (1, -1):
        src, dst, i = (248, 8, 0) if dx == 1 else (0, 272, 2)
        coef_sends.append(((dx, 0), [
            remote(dx, 0, trans.at[:, pl.ds(src, 8), :], tr.at[:, pl.ds(dst, 8), :], i),
            remote(dx, 0, reaction.at[pl.ds(src, 8), :], re.at[pl.ds(dst, 8), :], i + 1),
        ]))
        start(*coef_sends[-1])
    for dx in (0, 1, -1):
        for dy, side in ((1, 0), (-1, 1)):
            at, n = {0: (8, 48), 1: (0, 8), -1: (56, 8)}[dx]
            i = 4 + {0: 0, 1: 1, -1: 2}[dx] * 2 + side
            coef_sends.append(((dx, dy), [
                remote(dx, dy, yc.at[side, pl.ds(at, n), :], yd.at[side, pl.ds(at, n), :], i)
            ]))
            start(*coef_sends[-1])
    def y_send(dx, dy, side):
        at, n = {0: (40, 312), 1: (0, 40), -1: (352, 40)}[dx]
        i = 14 + {0: 0, 1: 1, -1: 2}[dx] * 2 + side
        cs = [remote(dx, dy, ys.at[side, pl.ds(at, n), :], yl.at[side, pl.ds(at, n), :], i)]
        (sends if dx else side_sends).append(((dx, dy), cs))
        start((dx, dy), cs)

    side_sends = []
    y_send(0, 1, 0)
    y_send(0, -1, 1)
    for dx in (1, -1):
        j, lo, px, at, i = (3, 92, 1, 12, 10) if dx == 1 else (0, 0, 0, 240, 12)
        sends.append(((dx, 0), [
            remote(dx, 0, basis.at[j, :, pl.ds(lo, 36), :], va.at[px, pl.ds(0, 4), pl.ds(at, 36), :], i),
            remote(dx, 0, support.at[j, :, pl.ds(lo, 36), :], sup.at[px, :, pl.ds(at, 36), :], i + 1),
        ]))
        start(*sends[-1])
    for dx in (1, -1):
        y_send(dx, 1, 0)
        y_send(dx, -1, 1)
    goals = []
    for n in range(1, NGX):
        goals.append(pltpu.make_async_remote_copy(
            tg.at[gx], tg.at[gx], sg.at[n], rg.at[n],
            device_id=((gx + n) % NGX, gy), device_id_type=MESH,
        ))

    for c in loads[n_first:]:
        c.wait()

    low_x, high_x = gx == 0, gx == NGX - 1
    low_y, high_y = gy == 0, gy == NGY - 1

    def classify(i, _):
        r = pl.ds(pl.multiple_of(i * 8 + 16, 8), 8)
        h = i // 4
        thx = jnp.where((h == 0) | (h == 3) | (h == 4), 3, 6)
        thx = jnp.where((h == 0) & low_x, 6, thx)
        thx = jnp.where((h == 7) & high_x, 3, thx)
        got = []
        for k in range(4):
            c = cod[k, r, :]
            cy = c - 3 * (jnp.where(c >= 3, 1, 0) + jnp.where(c >= 6, 1, 0))
            thl = jnp.where(low_y, 2, 1) if k == 0 else 1
            thr = jnp.where(high_y, 1, 2) if k == 3 else 2
            thy = jnp.where(right, thr, thl)
            v = jnp.where(c >= thx, 2, 0) + jnp.where(cy >= thy, 1, 0)
            got.append(jnp.where(act[k, r, :] > 0, v, 4))
        k4 = jnp.where(right, flip(got[0]), flip(got[3]))
        cls[0, r, :] = jnp.where(lane >= 32, got[0], 4)
        cls[1, r, :] = got[1]
        cls[2, r, :] = got[2]
        cls[3, r, :] = jnp.where(lane < 96, got[3], 4)
        cls[4, r, :] = jnp.where((lane < 32) | (lane >= 96), k4, 4)
        return 0

    lax.fori_loop(0, 32, classify, 0, unroll=4)

    def arrived(copies):
        for (dx, dy), cs in copies:
            @pl.when(exists(-dx, -dy))
            def _(cs=cs):
                for c in cs:
                    c.wait_recv()

    def spread(t0, t1):
        r0, l0, r1, l1 = roll(t0, 32), roll(t0, -32), roll(t1, 32), roll(t1, -32)
        k0 = jnp.where(lane < 32, 0.0, r0)
        k1 = jnp.where(lane < 96, l0, l1)
        k2 = jnp.where(lane < 32, r0, r1)
        k3 = jnp.where(lane < 96, l1, 0.0)
        return [k0, k1, k2, k3, jnp.where(right, flip(k0), flip(k3))]

    def widen(i, _):
        r = pl.ds(pl.multiple_of(i * 8 + 8, 8), 8)
        cx = spread(tr[0, r, 0:128], tr[0, r, 128:256])
        cy = spread(tr[1, r, 0:128], tr[1, r, 128:256])
        cr = spread(re[r, 0:128], re[r, 128:256])
        for kt in range(5):
            tx[kt, r, :] = cx[kt]
            ty[kt, r, :] = cy[kt]
            dg[kt, r, :] = cr[kt]
        return 0

    def dead(i, _):
        r = pl.ds(pl.multiple_of(i * 8 + 8, 8), 8)
        live = [act[k, r, :].astype(F32) for k in range(4)]
        live.append(jnp.where(right, flip(live[0]), flip(live[3])))
        for kt in range(5):
            ia[kt, r, :] = 1.0 - live[kt]
        return 0

    def diagonal(lo, hi, kts, unroll):
        own = (lo < 29, lo >= 5)

        def body(i, _):
            r = pl.ds(pl.multiple_of(i * 8 + 8, 8), 8)
            for kt in kts:
                w = pltpu.roll(ty[kt, r, :], 1, 1)
                tyw[kt, r, :] = w
                d = dg[kt, r, :] + tx[kt, r, :] + tx[kt, pl.ds(i * 8 + 7, 8), :] + ty[kt, r, :] + w
                dg[kt, r, :] = d
                inv = pl.reciprocal(jnp.maximum(d, 0.005), approx=True)
                inv = inv * (2.0 - jnp.maximum(d, 0.005) * inv)
                wd = (OMEGA * inv) * (1.0 - ia[kt, r, :])
                for px in range(2):
                    if kt < 4 and own[px]:
                        kd[px, kt, r, :] = wd * sup[px, kt, r, :].astype(F32)
                    else:
                        kd[px, kt, r, :] = wd
            return 0

        lax.fori_loop(lo, hi, body, 0, unroll=unroll)

    lax.fori_loop(1, 33, widen, 0, unroll=2)
    lax.fori_loop(0, SLABS, dead, 0, unroll=2)
    diagonal(2, 5, (1, 2), 3)
    diagonal(5, 29, (1, 2), 4)
    diagonal(29, 33, (1, 2), 4)

    arrived(coef_sends)
    for c in goals:
        c.start()
    for at in (8, 272):
        re[at:at + 8, :] = re[at:at + 8, :] + tr[2, at:at + 8, :]
    widen(0, 0)
    widen(33, 0)
    for f, ref in enumerate((tx, ty, dg)):
        for n in range(SLABS):
            if n == 0 or n == SLABS - 1:
                at, away = (0 if n == 0 else 56), 8 * f
            else:
                h, i = divmod(n - 1, 16)
                at, away = 8 + (f * 2 + h) * 8, 8 * i
            x0, x1 = yd[0, at:at + 8, :], yd[1, at:at + 8, :]
            r = slice(8 * n + 8, 8 * n + 16)
            ref[0, r, :] = jnp.where((lane >= 24) & (lane < 32), roll(x0, 24 - away), ref[0, r, :])
            ref[3, r, :] = jnp.where((lane >= 96) & (lane < 104), roll(x1, 96 - away), ref[3, r, :])
            x = jnp.where((lane >= 88) & (lane < 96), roll(x0, 88 - away), ref[4, r, :])
            ref[4, r, :] = jnp.where((lane >= 32) & (lane < 40), roll(x1, 32 - away), x)
    diagonal(0, 2, (1, 2), 2)
    diagonal(33, 34, (1, 2), 1)
    diagonal(0, 5, (0, 3, 4), 5)
    diagonal(5, 29, (0, 3, 4), 4)
    diagonal(29, 34, (0, 3, 4), 5)

    def keep(first, px):
        def body(i, _):
            r = pl.ds(pl.multiple_of(i * 8 + first, 8), 8)
            for k in range(4):
                kd[px, k, r, :] = kd[px, k, r, :] * sup[px, k, r, :].astype(F32)
            return 0

        return body

    def flux_sum(v, px, kt, i):
        r = pl.ds(pl.multiple_of(i * 8 + 8, 8), 8)
        mid = v[px, kt, r, :]
        up = v[px, kt, pl.ds(i * 8 + 9, 8), :]
        dn = v[px, kt, pl.ds(i * 8 + 7, 8), :]
        total = (
            tx[kt, r, :] * up
            + tx[kt, pl.ds(i * 8 + 7, 8), :] * dn
            + ty[kt, r, :] * pltpu.roll(mid, 127, 1)
            + tyw[kt, r, :] * pltpu.roll(mid, 1, 1)
        )
        return mid, total

    def sweep(src, dst, starts, count, unroll):
        def first(i):
            r = pl.ds(pl.multiple_of(i * 8 + 8, 8), 8)
            raw = []
            for kt in range(5):
                for px in range(2):
                    mid, total = flux_sum(src, px, kt, i)
                    raw.append((1.0 - OMEGA) * mid + kd[px, kt, r, :] * total)
            turned = [flip(raw[2 * kt] + raw[2 * kt + 1]) for kt in range(5)]
            return tuple(raw), tuple(turned)

        def second(i, raw, turned):
            r = pl.ds(pl.multiple_of(i * 8 + 8, 8), 8)
            for kt in range(5):
                t = raw[2 * kt] + raw[2 * kt + 1]
                t = t + jnp.where(right, turned[(kt + 1) % 5], turned[(kt + 4) % 5])
                t = jnp.maximum(t + ia[kt, r, :], 1e-30)
                inv = pl.reciprocal(t, approx=True)
                inv = inv * (2.0 - t * inv)
                for px in range(2):
                    dst[px, kt, r, :] = raw[2 * kt + px] * inv

        def firsts(i):
            return tuple(first(n + i) for n in starts)

        def body(i, held):
            new = firsts(i)
            for n, h in zip(starts, held):
                second(n + i - 1, *h)
            return new

        held = lax.fori_loop(1, count, body, firsts(0), unroll=unroll)
        for n, h in zip(starts, held):
            second(n + count - 1, *h)

    fin = vb

    def image(h, _):
        for kt in range(5):
            acc = [None] * 8
            for s in range(4):
                i = h * 4 + s + 1
                r = pl.ds(pl.multiple_of(i * 8 + 8, 8), 8)
                c = cls[kt, r, :]
                pick = [c == q for q in range(4)]
                for px in range(2):
                    mid, total = flux_sum(fin, px, kt, i)
                    img = dg[kt, r, :] * mid - total
                    for q in range(4):
                        n = (q // 2) * 4 + px * 2 + q % 2
                        x = jnp.where(pick[q], img, 0.0)
                        acc[n] = x if acc[n] is None else acc[n] + x
            zz[h, kt] = fold_rows(acc)
        return 0


    def remote2(dx, dy, src, dst, i):
        return pltpu.make_async_remote_copy(
            src, dst, s2.at[i], r2.at[i], device_id=(gx + dx, gy + dy), device_id_type=MESH
        )

    late = ((1, 2, 3, 4, 5, 6, 7, 26, 27, 28), (5, 6, 7, 26, 27, 28, 29, 30, 31, 32))
    backs = []

    def put(side, at, places):
        m = None
        for g, (px, n) in enumerate(places):
            x = roll(fin[px, 4, 8 * n + 8:8 * n + 16, :], 32 * g if side == 0 else 32 * g + 32)
            m = x if m is None else jnp.where(lane < 32 * g, m, x)
        rs[side, at:at + 8, :] = m

    def back(dx, dy, src, dst, i):
        backs.append(((dx, dy), remote2(dx, dy, src, dst, i)))
        start((dx, dy), [backs[-1][1]])

    def back_side(dx, at, n, i):
        for dy, side in ((1, 0), (-1, 1)):
            back(dx, dy, rs.at[side, pl.ds(at, n), :], rl.at[side, pl.ds(at, n), :], i + side)

    early_places = [[(0, 8 + m), (0, 17 + m), (1, 8 + m), (1, 17 + m)] for m in range(9)]
    late_places = [[(0, late[0][m]), (0, late[0][m + 5]), (1, late[1][m]), (1, late[1][m + 5])] for m in range(5)]

    arrived(side_sends)

    def apart(m0, m1, n):
        return jnp.where(
            lane < 40, roll(m1, -40 * n), jnp.where(lane >= 88, roll(m0, 88 - 40 * n), 0.0)
        )

    def unpack(i, _):
        yr = pl.ds(pl.multiple_of(i * 8 + 40, 8), 8)
        even = pl.ds(pl.multiple_of(i * 8 + 8, 8), 8)
        odd = pl.ds(pl.multiple_of(i * 8 + 48, 8), 8)
        m0, m1 = yl[0, yr, :], yl[1, yr, :]
        va[0, 4, even, :] = apart(m0, m1, 0)
        va[1, 4, odd, :] = apart(m0, m1, 1)
        kd[0, 4, even, :] = kd[0, 4, even, :] * apart(m0, m1, 2)
        return 0

    lax.fori_loop(0, 29, unpack, 0, unroll=29)
    for i in range(10):
        m0, m1 = yl[0, 272 + 8 * i:280 + 8 * i, :], yl[1, 272 + 8 * i:280 + 8 * i, :]
        for n in range(3):
            at = 48 + 8 * (i + 10 * n)
            if i + 10 * n < 29:
                kd[1, 4, at:at + 8, :] = kd[1, 4, at:at + 8, :] * apart(m0, m1, n)

    sweep(va, vb, (6,), 22, 3)
    sweep(vb, va, (7,), 20, 3)
    sweep(va, vb, (8,), 18, 3)
    for side in range(2):
        for m in range(9):
            put(side, 8 + 8 * m, early_places[m])
    back_side(0, 8, 72, 0)
    lax.fori_loop(2, 6, image, 0)

    arrived(sends)
    lax.fori_loop(0, 5, keep(240, 0), 0, unroll=5)
    lax.fori_loop(0, 5, keep(8, 1), 0, unroll=5)
    for px, at, to in ((1, 0, 8), (0, 352, 240)):
        for n in range(5):
            m0, m1 = yl[0, at + 8 * n:at + 8 * n + 8, :], yl[1, at + 8 * n:at + 8 * n + 8, :]
            r = slice(to + 8 * n, to + 8 * n + 8)
            va[px, 4, r, :] = jnp.where(right, m0, m1)
            kd[px, 4, r, :] = kd[px, 4, r, :] * flip(jnp.where(right, m1, m0))

    sweep(va, vb, (0, 28), 6, 2)
    sweep(vb, va, (0, 27), 7, 2)
    sweep(va, vb, (0, 26), 8, 2)

    back(-1, 0, fin.at[1, pl.ds(0, 4), pl.ds(16, 32), :], out.at[3, :, pl.ds(96, 32), :], 2)
    back(1, 0, fin.at[0, pl.ds(0, 4), pl.ds(240, 32), :], out.at[0, :, pl.ds(0, 32), :], 3)
    for side in range(2):
        for m in range(5):
            put(side, 80 + 8 * m, late_places[m])
        put(side, 0, [(1, n) for n in range(1, 5)])
        put(side, 120, [(0, n) for n in range(29, 33)])
    back_side(0, 80, 40, 4)
    back_side(1, 120, 8, 6)
    back_side(-1, 0, 8, 8)

    lax.fori_loop(0, 2, image, 0, unroll=2)
    lax.fori_loop(6, 8, image, 0, unroll=2)

    table = jnp.zeros((8, 128), F32)
    bit_x, odd, bit_y = sub // 4, (sub // 2) % 2, sub % 2
    for a in range(5):
        part = jnp.zeros((8, 128), F32)
        base_x = a
        if a == 0:
            base_x = jnp.where(low_x, 1, 0)
        if a == 4:
            base_x = jnp.where(high_x, 3, 4)
        window_x = a - (a + odd) % 2
        dxo = window_x - (base_x - 1 + bit_x)
        for kt in range(5):
            z = zz[0, kt] if a == 0 else (zz[7, kt] if a == 4 else zz[2 * a - 1, kt] + zz[2 * a, kt])
            for shift in (32, 16, 8, 4, 2, 1):
                z = z + roll(z, -shift)
            for half in range(2):
                if kt < 4:
                    b, window_y = kt + half, kt
                else:
                    b, window_y = (4, 4) if half == 0 else (0, -1)
                base_y = b
                if b == 0:
                    base_y = jnp.where(low_y, 1, 0)
                if b == 4:
                    base_y = jnp.where(high_y, 3, 4)
                dyo = window_y - (base_y - 1 + bit_y)
                to = (base_y + bit_y) * 16 + (dxo + 1) * 3 + dyo + 1
                value = jnp.broadcast_to(z[:, 64 * half:64 * half + 1], (8, 128))
                part = part + jnp.where(lane == to, value, 0.0)
        low = jnp.sum(part[0:4], axis=0, keepdims=True)
        high = jnp.sum(part[4:8], axis=0, keepdims=True)
        table = table + jnp.where(sub == base_x, low, 0.0) + jnp.where(sub == base_x + 1, high, 0.0)
    tb[1, gx] = table * (1.0 / 64.0)

    hops = []
    for n, (s, t) in enumerate(peers):
        hops.append((t, pltpu.make_async_remote_copy(
            tb.at[1, gx], tb.at[1 - t, gx], st.at[n], rt.at[n],
            device_id=((gx + s) % NGX, gy + t), device_id_type=MESH,
        )))
    for t, c in hops:
        @pl.when(exists(0, t))
        def _(c=c):
            c.start()

    def emit(i, _):
        def one(j, px, first, to):
            for k in range(4):
                out[j, k, pl.ds(pl.multiple_of(to + i * 8, 8), 8), :] = fin[
                    px, k, pl.ds(pl.multiple_of(first + i * 8, 8), 8), :
                ]

        one(0, 0, 16, 32)
        one(1, 1, 48, 0)
        one(2, 0, 112, 0)
        one(3, 1, 176, 0)
        return 0

    lax.fori_loop(0, 12, emit, 0, unroll=4)
    for i in range(12, 16):
        for k in range(4):
            out[1, k, i * 8:i * 8 + 8, :] = fin[1, k, 48 + i * 8:56 + i * 8, :]
            out[2, k, i * 8:i * 8 + 8, :] = fin[0, k, 112 + i * 8:120 + i * 8, :]

    for (dx, dy), c in backs:
        @pl.when(exists(-dx, -dy))
        def _(c=c):
            c.wait_recv()

    for side, k in ((0, 0), (1, 3)):
        def merge(j, at, src, g):
            x = rl[side, pl.ds(src, 8), :]
            x = roll(x, -32 * g if side == 0 else 96 - 32 * g)
            inside = lane < 32 if side == 0 else lane >= 96
            out[j, k, at:at + 8, :] = jnp.where(inside, x, out[j, k, at:at + 8, :])

        for g in range(4):
            merge(0, 8 * g, 120, g)
            merge(3, 96 + 8 * g, 0, g)
        for first, places in ((8, early_places), (80, late_places)):
            for m, four in enumerate(places):
                for g, (px, n) in enumerate(four):
                    row = 8 * (n - 1)
                    if px == 0:
                        j, at = (0, row + 32) if row < 96 else (2, row - 96)
                    else:
                        j, at = (1, row - 32) if row < 160 else (3, row - 160)
                    merge(j, at, first + 8 * m, g)

    for t, c in hops:
        @pl.when(exists(0, -t))
        def _(c=c):
            c.wait_recv()

    for c in goals:
        c.wait_recv()

    joined = []
    for s in range(NGX):
        a = tb[1, s]
        below = roll(tb[0, s], -64)
        above = roll(tb[2, s], 64)
        group = lane // 16
        joined.append(a + jnp.where(group == 1, below, 0.0) + jnp.where(group == 4, above, 0.0))
    for s in range(NGX):
        t = joined[s]
        if s > 0:
            t = t + jnp.where(sub == 1, sroll(joined[s - 1], -4), 0.0)
        if s < NGX - 1:
            t = t + jnp.where(sub == 4, sroll(joined[s + 1], 4), 0.0)
        goal = tg[s]
        for q in range(4):
            mine = jnp.where(goal == (gx * 4 + q).astype(F32), t, 0.0)
            line = jnp.sum(mine, axis=0, keepdims=True)
            line = line + pltpu.roll(line, 96, 1)
            line = line + pltpu.roll(line, 112, 1)
            rows_out[s * 4 + q:s * 4 + q + 1, :] = line[:, 16:25]

    for (dx, dy), cs in coef_sends + side_sends + sends:
        @pl.when(exists(dx, dy))
        def _(cs=cs):
            for c in cs:
                c.wait_send()
    for (dx, dy), c in backs:
        @pl.when(exists(dx, dy))
        def _(c=c):
            c.wait_send()
    for t, c in hops:
        @pl.when(exists(0, t))
        def _(c=c):
            c.wait_send()
    for c in goals:
        c.wait_send()


def local(basis, trans, reaction, support, codes, active, owner):
    anywhere = pl.BlockSpec(memory_space=pltpu.HBM)
    vmem = pl.BlockSpec(memory_space=pltpu.VMEM)
    sem = pltpu.SemaphoreType.DMA
    smoothed, coarse = pl.pallas_call(
        kernel,
        name="smooth",
        out_shape=(
            pltpu.VMEM((4, 4, 128, 128), F32),
            pltpu.VMEM((32, 9), F32),
        ),
        in_specs=[anywhere] * 6 + [pl.BlockSpec(memory_space=pltpu.SMEM)],
        out_specs=(vmem, vmem),
        scratch_shapes=[
            pltpu.VMEM((2, 5, ROWS, 128), F32),
            pltpu.VMEM((2, 5, ROWS, 128), F32),
            pltpu.VMEM((2, 4, ROWS, 128), jnp.int32),
            pltpu.VMEM((4, ROWS, 128), jnp.int32),
            pltpu.VMEM((4, ROWS, 128), jnp.int32),
            pltpu.VMEM((3, ROWS, 256), F32),
            pltpu.VMEM((ROWS, 256), F32),
            pltpu.VMEM((5, ROWS, 128), F32),
            pltpu.VMEM((5, ROWS, 128), F32),
            pltpu.VMEM((5, ROWS, 128), F32),
            pltpu.VMEM((5, ROWS, 128), F32),
            pltpu.VMEM((2, 5, ROWS, 128), F32),
            pltpu.VMEM((5, ROWS, 128), F32),
            pltpu.VMEM((2, 4, 40, 128), F32),
            pltpu.VMEM((2, 4, 40, 128), jnp.int32),
            pltpu.VMEM((2, YROWS, 128), F32),
            pltpu.VMEM((2, YROWS, 128), F32),
            pltpu.VMEM((2, CROWS, 128), F32),
            pltpu.VMEM((2, CROWS, 128), F32),
            pltpu.VMEM((2, 128, 128), F32),
            pltpu.VMEM((2, 128, 128), F32),
            pltpu.VMEM((3, NGX, 8, 128), F32),
            pltpu.VMEM((NGX, 8, 128), F32),
            pltpu.VMEM((5, ROWS, 128), jnp.int32),
            pltpu.VMEM((8, 5, 8, 128), F32),
            sem((32,)), sem((24,)), sem((24,)), sem((10,)), sem((10,)), sem((24,)), sem((24,)), sem((8,)), sem((8,)),
        ],
        compiler_params=pltpu.CompilerParams(
            collective_id=0, has_side_effects=True, vmem_limit_bytes=60 << 20
        ),
    )(basis[0], trans[:, 0], reaction[0], support, codes, active[0], owner.reshape(16))
    return smoothed[None], coarse


def solution(mesh):
    return jax.shard_map(
        local,
        mesh=mesh,
        in_specs=(
            P(None, "gx", "gy", None, None),
            P(None, None, "gx", "gy"),
            P(None, "gx", "gy"),
            P("gx", "gy", None, None),
            P("gx", "gy", None, None),
            P(None, "gx", "gy", None, None),
            P(("gx", "gy"), None),
        ),
        out_specs=(P(None, "gx", "gy", None, None), P(("gx", "gy"), None)),
        check_vma=False,
    )
```
